256 devices in a mesh: head: 8 (over z), seq: 32 (over x, y, core).
Axes of the slice: x: 4, y: 4, z: 8, core: 2. Of those that a mesh axis runs over, the one named last changes fastest.
Arguments:
- q_routed: bfloat16 [8, 32768, 128], P('head', 'seq'), may hold values from -8 to 8
- k_routed: bfloat16 [8, 32768, 128], P('head', 'seq'), may hold values from -8 to 8
- v_routed: bfloat16 [8, 32768, 128], P('head', 'seq'), may hold values from -6 to 6
- memberships: int32 [8, 32768, 1], P('head', 'seq'), may hold values from 0 to 31; in each aligned block of 1024 rows (0 to 1023, 1024 to 2047, ..., all dimensions but the last counted through in order) at most 128 rows name the same one
- q_local: bfloat16 [8, 32768, 128], P('head', 'seq'), may hold values from -8 to 8
- k_local: bfloat16 [8, 32768, 128], P('head', 'seq'), may hold values from -8 to 8
- v_local: bfloat16 [8, 32768, 128], P('head', 'seq'), may hold values from -6 to 6
Outputs:
- out_routed: bfloat16 [8, 32768, 128], P('head', 'seq')
- out_local: bfloat16 [8, 32768, 128], P('head', 'seq')
The draws below stay inside these ranges and needn't reach their ends.
Inputs may be any that keep to these rules, and one draw needn't show every extreme that they name: `memberships`: in each head, the 1024 tokens of one sequence block name any one cluster at most 128 times, a bound that some block reaches.
All inputs are finite; a program needn't handle non-finite values.
Results may differ from the reference program's by a relative error of at most 0.0049.
Values may be sent and summed in bfloat16 or wider, within the bound.
No kernel may reach another device: no remote copies, remote signals or barrier semaphores. Data moves between devices by JAX's collectives and lax.ppermute only.
A program may use at most 64 MiB of HBM per device.

```python
import math
import jax
import jax.numpy as jnp
import numpy as np
from jax import lax

D_HEAD = 128
HALF = 8
CLUSTERS = 32
WIN = 2048
TOK_DEV = 1024
CAP = 128
SEQLEN = 32768
N_SEQ = 32


def pair_draw(key, tag):
    base = jax.random.fold_in(key, tag)
    streams = jax.random.split(base, 3)
    shape = (HALF, SEQLEN, D_HEAD)
    row_scales = jnp.exp(jax.random.uniform(streams[0], (HALF, SEQLEN, 1), jnp.float32, math.log(0.3), math.log(3.0)))
    queries = jax.random.normal(streams[1], shape, jnp.float32) * row_scales
    keys_out = jax.random.normal(streams[2], shape, jnp.float32)
    return (jnp.clip(queries, -8.0, 8.0), jnp.clip(keys_out, -8.0, 8.0))


def draw_q_routed(key, part):
    return pair_draw(key, 11)[0].astype(jnp.bfloat16)


def draw_k_routed(key, part):
    return pair_draw(key, 11)[1].astype(jnp.bfloat16)


def draw_q_local(key, part):
    return pair_draw(key, 23)[0].astype(jnp.bfloat16)


def draw_k_local(key, part):
    return pair_draw(key, 23)[1].astype(jnp.bfloat16)


def block_scale(own_key, dims, cuts, least, largest):
    factor_of = 1.0
    for axis_at, parts in cuts:
        heights = jax.random.uniform(jax.random.fold_in(jax.random.fold_in(own_key, 6), axis_at), (parts,), jnp.float32, least / len(cuts), largest / len(cuts))
        factor_of = factor_of * jnp.repeat(jnp.exp(heights), dims[axis_at] // parts).reshape((-1,) + (1,) * (len(dims) - 1 - axis_at))
    return factor_of


def shared_out(stream_key, own, number, rows, count, top, limit, skew):
    order = jax.random.permutation(stream_key, count)
    heavy_load, ordinary = portions_of(count, rows * top, limit, skew, True), portions_of(count, rows * top, limit, skew, False)
    places = jnp.arange(count)

    def named(lengths, turn):
        used = int((lengths > 0).sum())
        fixed = max(1, used // 4)
        shifted = fixed + (places - fixed + turn * (used - fixed)) % max(1, count - fixed)
        return jnp.zeros((count,), jnp.int32).at[order[jnp.where(places < fixed, places, shifted)]].set(jnp.asarray(lengths, jnp.int32))

    lengths = jnp.where(number % 4 == 0, named(heavy_load, number // 4), named(ordinary, number - number // 4 - 1))
    mixed = jax.random.permutation(jax.random.fold_in(own, 3), count)
    donor, sink = mixed[0:count // 2 * 2:2], mixed[1:count // 2 * 2:2]
    slack = jnp.minimum(lengths[donor] - 1, limit - lengths[sink]) // 2
    slack = jnp.where((donor == order[0]) | (sink == order[0]) | (lengths[sink] == 0), 0, jnp.maximum(slack, 0))
    shifted = jax.random.randint(jax.random.fold_in(own, 4), (count // 2,), 0, 1 << 20) % (slack + 1)
    lengths = lengths.at[donor].add(-shifted).at[sink].add(shifted)
    items = jnp.searchsorted(jnp.cumsum(lengths), jnp.arange(rows * top), side="right").astype(jnp.int32)
    grid = items.reshape(top, rows).T
    grid = grid[jax.random.permutation(jax.random.fold_in(own, 1), rows)]
    turn = jax.random.randint(jax.random.fold_in(own, 2), (rows, 1), 0, top)
    return jnp.take_along_axis(grid, (jnp.arange(top)[None, :] + turn) % top, axis=1)


def portions_of(number_of, total, reach, slope, full):
    loads = [(1 << 20) // math.isqrt(rank ** slope) + 1 for rank in range(1, number_of + 1)]
    largest = reach if full else min(reach, max(-(-total // number_of), total * loads[0] // sum(loads)))
    least = 1 if total - largest >= number_of - 1 else 0
    counts, rest = [largest] + [least] * (number_of - 1), total - largest - least * (number_of - 1)
    while rest > 0:
        movable = [i for i in range(1, number_of) if counts[i] < largest] or [i for i in range(1, number_of) if counts[i] < reach]
        pool, budget = sum([loads[i] for i in movable]), rest
        for i in movable:
            extra = min(reach - counts[i], max(1, budget * loads[i] // pool), rest)
            counts[i] = counts[i] + extra
            rest = rest - extra
    return np.array(counts)


def scatter_about(stream_key, extent, deviation, reach, pieces=(), kind=jnp.bfloat16):
    array = jax.random.normal(stream_key, extent, jnp.float32) * deviation
    if len(pieces) > 0:
        array = block_scale(stream_key, extent, pieces, -0.22, 0.18) * array
    return jnp.clip(array, min=-reach, max=reach).astype(kind)


def setup_inputs(seed: int = 0) -> dict:
    keys = jax.random.split(jax.random.key(seed), 8)
    q_routed = draw_q_routed(jax.random.fold_in(keys[7], 71), 0)
    k_routed = draw_k_routed(jax.random.fold_in(keys[7], 71), 0)
    v_routed = scatter_about(keys[2], (HALF, SEQLEN, D_HEAD), 1.0, 6.0, ((0, 8), (1, 32)))
    memberships_keys = jax.random.split(jax.random.fold_in(keys[3], 1), HALF * SEQLEN // TOK_DEV)
    memberships_turns = jax.random.permutation(jax.random.fold_in(keys[3], 3), HALF * SEQLEN // TOK_DEV)
    memberships = jax.vmap(lambda own, number: shared_out(jax.random.fold_in(keys[3], 2), own, number, TOK_DEV, CLUSTERS, 1, CAP, 2))(memberships_keys, memberships_turns).reshape((HALF, SEQLEN, 1))
    q_local = draw_q_local(jax.random.fold_in(keys[7], 71), 0)
    k_local = draw_k_local(jax.random.fold_in(keys[7], 71), 0)
    v_local = scatter_about(keys[6], (HALF, SEQLEN, D_HEAD), 1.0, 6.0, ((0, 8), (1, 32)))
    return {"q_routed": q_routed, "k_routed": k_routed, "v_routed": v_routed, "memberships": memberships, "q_local": q_local, "k_local": k_local, "v_local": v_local}


def mix_rows(scores, allowed, value_rows):
    scores = jnp.where(allowed, scores, -1e30)
    row_max = jnp.max(scores, axis=-1, keepdims=True)
    exponent = jnp.exp(scores - row_max)
    row_total = jnp.sum(exponent, axis=-1, keepdims=True)
    weights = (exponent / row_total).astype(jnp.bfloat16)
    mixed = jnp.dot(weights.astype(jnp.float32), value_rows.astype(jnp.float32), preferred_element_type=jnp.float32)
    return mixed.astype(jnp.bfloat16)


def block_scores(query_block, key_block):
    score_scale = D_HEAD ** -0.5
    return jnp.dot(query_block.astype(jnp.float32), key_block.astype(jnp.float32).T, preferred_element_type=jnp.float32) * score_scale


def routed_head(inputs):
    queries, keys_in, values_in, cluster_ids = inputs
    positions = jnp.arange(SEQLEN, dtype=jnp.int32)
    order = jnp.argsort(cluster_ids * SEQLEN + positions).astype(jnp.int32)
    sorted_q = queries[order]
    sorted_ids = cluster_ids[order]
    sorted_pos = positions[order]
    reach_rows = N_SEQ * CAP
    pad_keys = jnp.concatenate([jnp.zeros((reach_rows, D_HEAD), keys_in.dtype), keys_in[order]], axis=0)
    pad_values = jnp.concatenate([jnp.zeros((reach_rows, D_HEAD), values_in.dtype), values_in[order]], axis=0)
    pad_ids = jnp.concatenate([jnp.full((reach_rows,), -1, jnp.int32), sorted_ids], axis=0)
    pad_pos = jnp.concatenate([jnp.zeros((reach_rows,), jnp.int32), sorted_pos], axis=0)
    block_rows = min(512, SEQLEN)

    def one_block(block_index):
        first_row = (block_index * block_rows).astype(jnp.int32)
        query_block = lax.dynamic_slice_in_dim(sorted_q, first_row, block_rows, 0)
        query_ids = lax.dynamic_slice_in_dim(sorted_ids, first_row, block_rows, 0)
        query_pos = lax.dynamic_slice_in_dim(sorted_pos, first_row, block_rows, 0)
        key_block = lax.dynamic_slice_in_dim(pad_keys, first_row, reach_rows + block_rows, 0)
        value_block = lax.dynamic_slice_in_dim(pad_values, first_row, reach_rows + block_rows, 0)
        id_block = lax.dynamic_slice_in_dim(pad_ids, first_row, reach_rows + block_rows, 0)
        pos_block = lax.dynamic_slice_in_dim(pad_pos, first_row, reach_rows + block_rows, 0)
        allowed = (id_block[None, :] == query_ids[:, None]) & (pos_block[None, :] <= query_pos[:, None])
        return mix_rows(block_scores(query_block, key_block), allowed, value_block)

    mixed = lax.map(one_block, jnp.arange(SEQLEN // block_rows, dtype=jnp.int32)).reshape(SEQLEN, D_HEAD)
    return jnp.zeros_like(mixed).at[order].set(mixed)


def local_head(inputs):
    queries, keys_in, values_in = inputs
    pad_keys = jnp.concatenate([jnp.zeros((WIN, D_HEAD), keys_in.dtype), keys_in], axis=0)
    pad_values = jnp.concatenate([jnp.zeros((WIN, D_HEAD), values_in.dtype), values_in], axis=0)
    block_rows = min(512, SEQLEN)

    def one_block(block_index):
        first_row = (block_index * block_rows).astype(jnp.int32)
        query_block = lax.dynamic_slice_in_dim(queries, first_row, block_rows, 0)
        key_block = lax.dynamic_slice_in_dim(pad_keys, first_row, WIN + block_rows, 0)
        value_block = lax.dynamic_slice_in_dim(pad_values, first_row, WIN + block_rows, 0)
        query_pos = first_row + jnp.arange(block_rows, dtype=jnp.int32)
        key_pos = first_row - WIN + jnp.arange(WIN + block_rows, dtype=jnp.int32)
        distance_back = query_pos[:, None] - key_pos[None, :]
        allowed = (key_pos[None, :] >= 0) & (distance_back >= 0) & (distance_back < WIN)
        return mix_rows(block_scores(query_block, key_block), allowed, value_block)

    return lax.map(one_block, jnp.arange(SEQLEN // block_rows, dtype=jnp.int32)).reshape(SEQLEN, D_HEAD)


def reference(q_routed, k_routed, v_routed, memberships, q_local, k_local, v_local):
    out_routed = lax.map(routed_head, (q_routed, k_routed, v_routed, memberships[:, :, 0]))
    out_local = lax.map(local_head, (q_local, k_local, v_local))
    return (out_routed, out_local)
```

```python
import jax
import jax.numpy as jnp
from jax import lax
from jax.experimental import pallas as pl
from jax.experimental.pallas import tpu as pltpu
from jax.sharding import Mesh
from jax.sharding import PartitionSpec as P

CLUSTERS = 32
CAP = 128
TOK = 1024
D = 128
SEQ = ("seq_0", "seq_1", "seq_2")
LOG2E = 1.4426950408889634
EXP_SCALE = LOG2E * D**-0.5
NEVER = -1e30
EMPTY = 256.0
GROUP = 8
VMEM = pl.BlockSpec(memory_space=pltpu.VMEM)


def params():
    return pltpu.CompilerParams(vmem_limit_bytes=56 * 1024 * 1024)


def pack_kernel(ids_ref, q_ref, k_ref, v_ref, sent_ref, rank_ref):
    ids = ids_ref[...]
    member = (ids == lax.broadcasted_iota(jnp.int32, (CLUSTERS, TOK), 0)).astype(jnp.float32)
    member_b = member.astype(jnp.bfloat16)
    upto = (
        lax.broadcasted_iota(jnp.int32, (128, 128), 0)
        <= lax.broadcasted_iota(jnp.int32, (128, 128), 1)
    ).astype(jnp.bfloat16)
    count = jnp.zeros((CLUSTERS, 1), jnp.float32)
    ranks = []
    for first in range(0, TOK, 128):
        seen = count + jnp.dot(
            member_b[:, first : first + 128], upto, preferred_element_type=jnp.float32
        )
        ranks.append(
            jnp.sum(member[:, first : first + 128] * seen, axis=0, keepdims=True) - 1.0
        )
        count = seen[:, 127:128]
    rank = jnp.concatenate(ranks, axis=1)
    rank_ref[...] = jnp.broadcast_to(rank, rank_ref.shape)
    at_rank = (
        rank.astype(jnp.int32) == lax.broadcasted_iota(jnp.int32, (CAP, TOK), 0)
    ).astype(jnp.bfloat16)
    rows = jnp.concatenate([q_ref[...], k_ref[...], v_ref[...]], axis=1)
    slot = lax.broadcasted_iota(jnp.int32, (CAP, D), 0).astype(jnp.float32)
    for base in range(0, CLUSTERS, GROUP):
        place = jnp.concatenate(
            [at_rank * member_b[c : c + 1] for c in range(base, base + GROUP)], axis=0
        )
        placed = jnp.dot(place, rows, preferred_element_type=jnp.float32)
        for i in range(GROUP):
            c = base + i
            mine = placed[i * CAP : (i + 1) * CAP]
            sent_ref[c, 0:CAP] = mine[:, 0:D].astype(jnp.bfloat16)
            used = slot < jnp.broadcast_to(count[c : c + 1], (CAP, D))
            sent_ref[c, CAP : 2 * CAP] = jnp.where(used, mine[:, D : 2 * D], EMPTY).astype(
                jnp.bfloat16
            )
            sent_ref[c, 2 * CAP : 3 * CAP] = mine[:, 2 * D : 3 * D].astype(jnp.bfloat16)


def pack(ids, q, k, v):
    return pl.pallas_call(
        pack_kernel,
        out_shape=(
            jax.ShapeDtypeStruct((CLUSTERS, 3 * CAP, D), jnp.bfloat16),
            jax.ShapeDtypeStruct((8, TOK), jnp.float32),
        ),
        in_specs=[VMEM] * 4,
        out_specs=(VMEM, VMEM),
        compiler_params=params(),
        name="pack_slots",
    )(ids, q, k, v)


def attend(queries, keys, values, allowed_of):
    scores = []
    for piece, allowed in zip(keys, allowed_of):
        s = lax.dot_general(
            queries, piece, (((1,), (1,)), ((), ())), preferred_element_type=jnp.float32
        )
        scores.append(s if allowed is None else jnp.where(allowed, s, NEVER))
    top = jnp.max(scores[0], axis=1, keepdims=True)
    for s in scores[1:]:
        top = jnp.maximum(top, jnp.max(s, axis=1, keepdims=True))
    shift = top * EXP_SCALE
    total = None
    for s, piece in zip(scores, values):
        weight = jnp.exp2(s * EXP_SCALE - shift).astype(jnp.bfloat16)
        part = jnp.dot(weight, piece, preferred_element_type=jnp.float32)
        total = part if total is None else total + part
    mass = total[:, D : 2 * D]
    return (total[:, 0:D] / jnp.where(mass > 0.0, mass, 1.0)).astype(jnp.bfloat16)


def routed_kernel(got_ref, out_ref, key_ref, value_ref):
    blocks = got_ref.shape[0]
    first = jnp.zeros((1, D), jnp.float32)
    for s in reversed(range(blocks)):
        row = got_ref[s, CAP : CAP + 16].astype(jnp.float32)[0:1]
        first = jnp.where(row < 100.0, row, first)
    filler = jnp.broadcast_to(first, (CAP, D))
    for s in range(blocks):
        key = got_ref[s, CAP : 2 * CAP].astype(jnp.float32)
        used = key < 100.0
        key_ref[s * CAP : (s + 1) * CAP] = jnp.where(used, key, filler).astype(jnp.bfloat16)
        value_ref[s * CAP : (s + 1) * CAP, 0:D] = got_ref[s, 2 * CAP : 3 * CAP]
        value_ref[s * CAP : (s + 1) * CAP, D : 2 * D] = used.astype(jnp.float32).astype(
            jnp.bfloat16
        )
    size = 2 * CAP
    within = lax.broadcasted_iota(jnp.int32, (size, size), 1) <= lax.broadcasted_iota(
        jnp.int32, (size, size), 0
    )
    for i in range(blocks // 2):
        low = i * size
        queries = got_ref[2 * i : 2 * i + 2, 0:CAP].reshape(size, D)
        keys, values, masks = [], [], []
        if low > 0:
            keys.append(key_ref[0:low])
            values.append(value_ref[0:low])
            masks.append(None)
        keys.append(key_ref[low : low + size])
        values.append(value_ref[low : low + size])
        masks.append(within)
        out_ref[2 * i : 2 * i + 2] = attend(queries, keys, values, masks).reshape(2, CAP, D)


def routed(got):
    blocks = got.shape[0]
    slots = blocks * CAP
    return pl.pallas_call(
        routed_kernel,
        out_shape=jax.ShapeDtypeStruct((blocks, CAP, D), jnp.bfloat16),
        in_specs=[VMEM],
        out_specs=VMEM,
        scratch_shapes=[
            pltpu.VMEM((slots, D), jnp.bfloat16),
            pltpu.VMEM((slots, 2 * D), jnp.bfloat16),
        ],
        compiler_params=params(),
        cost_estimate=pl.CostEstimate(
            flops=2 * slots * slots * D * 2, bytes_accessed=4 * slots * D * 2, transcendentals=0
        ),
        name="cluster_attention",
    )(got)


def local_kernel(at_ref, q_ref, k_ref, v_ref, far_ref, near_ref, out_ref, key_ref, value_ref):
    at = at_ref[0]
    own = k_ref[0:16].astype(jnp.float32)[0:1]
    nearest = near_ref[0, 0:16].astype(jnp.float32)[0:1]
    for b, ref in enumerate((far_ref, near_ref)):
        there = at >= 2 - b
        start = jnp.where(at == 0, own, nearest)
        filler = jnp.broadcast_to(start, (TOK, D))
        rows = pl.ds(b * TOK, TOK)
        key_ref[rows] = jnp.where(there, ref[0].astype(jnp.float32), filler).astype(jnp.bfloat16)
        value_ref[rows, 0:D] = ref[1]
        value_ref[rows, D : 2 * D] = jnp.full((TOK, D), jnp.where(there, 1.0, 0.0)).astype(
            jnp.bfloat16
        )
    key_ref[2 * TOK : 3 * TOK] = k_ref[...]
    value_ref[2 * TOK : 3 * TOK, 0:D] = v_ref[...]
    value_ref[2 * TOK : 3 * TOK, D : 2 * D] = jnp.ones((TOK, D), jnp.bfloat16)
    size = 256
    column = lax.broadcasted_iota(jnp.int32, (size, size), 1)
    line = lax.broadcasted_iota(jnp.int32, (size, size), 0)
    for i in range(TOK // size):
        low = i * size
        high = low + 2 * TOK
        spans = ((low, low + size), (low + size, high), (high, high + size))
        out_ref[low : low + size] = attend(
            q_ref[low : low + size],
            [key_ref[a:b] for a, b in spans],
            [value_ref[a:b] for a, b in spans],
            (column > line, None, column <= line),
        )


def windowed(at, q, k, v, far, near):
    return pl.pallas_call(
        local_kernel,
        out_shape=jax.ShapeDtypeStruct((TOK, D), jnp.bfloat16),
        in_specs=[pl.BlockSpec(memory_space=pltpu.SMEM)] + [VMEM] * 5,
        out_specs=VMEM,
        scratch_shapes=[
            pltpu.VMEM((3 * TOK, D), jnp.bfloat16),
            pltpu.VMEM((3 * TOK, 2 * D), jnp.bfloat16),
        ],
        compiler_params=params(),
        cost_estimate=pl.CostEstimate(
            flops=TOK * 2304 * D * 4, bytes_accessed=8 * TOK * D * 2, transcendentals=0
        ),
        name="window_attention",
    )(at, q, k, v, far, near)


def slot_kernel(ids_ref, rank_ref, at_rank_ref, ids_col_ref):
    rank = jnp.broadcast_to(rank_ref[0:1], (D, TOK)).T
    lane = lax.broadcasted_iota(jnp.int32, (TOK, CAP), 1)
    at_rank_ref[...] = (rank.astype(jnp.int32) == lane).astype(jnp.bfloat16)
    ids = jnp.broadcast_to(ids_ref[...].astype(jnp.float32), (D, TOK)).T
    ids_col_ref[...] = ids.astype(jnp.bfloat16)


def slots(ids, rank):
    return pl.pallas_call(
        slot_kernel,
        out_shape=(
            jax.ShapeDtypeStruct((TOK, CAP), jnp.bfloat16),
            jax.ShapeDtypeStruct((TOK, CAP), jnp.bfloat16),
        ),
        in_specs=[VMEM] * 2,
        out_specs=(VMEM, VMEM),
        compiler_params=params(),
        name="slot_columns",
    )(ids, rank)


def unpack_kernel(at_rank_ref, ids_ref, back_ref, out_ref):
    rows = 256
    for low in range(0, TOK, rows):
        at_rank = at_rank_ref[low : low + rows]
        ids = ids_ref[low : low + rows]
        zero = jnp.zeros_like(at_rank)
        picks = [
            jnp.where(ids == jnp.asarray(c, jnp.bfloat16), at_rank, zero) for c in range(CLUSTERS)
        ]
        pick = jnp.concatenate(picks, axis=1)
        out_ref[low : low + rows] = jnp.dot(
            pick, back_ref[...], preferred_element_type=jnp.float32
        ).astype(jnp.bfloat16)


def unpack(at_rank, ids_col, back):
    return pl.pallas_call(
        unpack_kernel,
        out_shape=jax.ShapeDtypeStruct((TOK, D), jnp.bfloat16),
        in_specs=[VMEM] * 3,
        out_specs=VMEM,
        compiler_params=params(),
        name="unpack_slots",
    )(at_rank, ids_col, back)


def passed_along(value, steps):
    count = lax.axis_size(SEQ)
    return lax.ppermute(value, SEQ, [(s, s + steps) for s in range(count - steps)])


def local(q_routed, k_routed, v_routed, memberships, q_local, k_local, v_local):
    seq_index = lax.axis_index(SEQ)
    pair = jnp.concatenate([k_local, v_local], axis=0)
    far = passed_along(pair, 2)
    near = passed_along(pair, 1)
    ids = memberships.reshape(1, TOK)
    sent, rank = pack(ids, q_routed[0], k_routed[0], v_routed[0])
    got = lax.all_to_all(sent, SEQ, split_axis=0, concat_axis=0, tiled=True)
    at_rank, ids_col = slots(ids, rank)
    out_local = windowed(
        seq_index.astype(jnp.int32).reshape(1), q_local[0], k_local[0], v_local[0], far, near
    )
    mixed = routed(got)
    back = lax.all_to_all(mixed, SEQ, split_axis=0, concat_axis=0, tiled=True)
    out_routed = unpack(at_rank, ids_col, back.reshape(CLUSTERS * CAP, D))
    return (out_routed[None], out_local[None])


def solution(mesh):
    torus = Mesh(
        mesh.devices.reshape(mesh.shape["head"], 4, 4, 2), ("head", "seq_0", "seq_1", "seq_2")
    )
    spec = P("head", SEQ, None)
    return jax.shard_map(
        local,
        mesh=torus,
        in_specs=(spec,) * 7,
        out_specs=(spec, spec),
        check_vma=False,
    )
```

```python
import jax
import jax.numpy as jnp
from jax import lax
from jax.experimental import pallas as pl
from jax.experimental.pallas import tpu as pltpu
from jax.sharding import Mesh
from jax.sharding import PartitionSpec as P

CLUSTERS = 32
CAP = 128
TOK = 1024
D = 128
SEQ = ("seq_0", "seq_1", "seq_2")
LOG2E = 1.4426950408889634
EXP_SCALE = LOG2E * D**-0.5
NEVER = -1e30
EMPTY = 256.0
GROUP = 8
VMEM = pl.BlockSpec(memory_space=pltpu.VMEM)


def params():
    return pltpu.CompilerParams(vmem_limit_bytes=56 * 1024 * 1024)


def pack_kernel(ids_ref, q_ref, k_ref, v_ref, sent_ref, rank_ref):
    ids = ids_ref[...]
    member = (ids == lax.broadcasted_iota(jnp.int32, (CLUSTERS, TOK), 0)).astype(jnp.float32)
    member_b = member.astype(jnp.bfloat16)
    upto = (
        lax.broadcasted_iota(jnp.int32, (128, 128), 0)
        <= lax.broadcasted_iota(jnp.int32, (128, 128), 1)
    ).astype(jnp.bfloat16)
    count = jnp.zeros((CLUSTERS, 1), jnp.float32)
    ranks = []
    for first in range(0, TOK, 128):
        seen = count + jnp.dot(
            member_b[:, first : first + 128], upto, preferred_element_type=jnp.float32
        )
        ranks.append(
            jnp.sum(member[:, first : first + 128] * seen, axis=0, keepdims=True) - 1.0
        )
        count = seen[:, 127:128]
    rank = jnp.concatenate(ranks, axis=1)
    rank_ref[...] = jnp.broadcast_to(rank, rank_ref.shape)
    at_rank = (
        rank.astype(jnp.int32) == lax.broadcasted_iota(jnp.int32, (CAP, TOK), 0)
    ).astype(jnp.bfloat16)
    rows = jnp.concatenate([q_ref[...], k_ref[...], v_ref[...]], axis=1)
    slot = lax.broadcasted_iota(jnp.int32, (CAP, D), 0).astype(jnp.float32)
    for base in range(0, CLUSTERS, GROUP):
        place = jnp.concatenate(
            [at_rank * member_b[c : c + 1] for c in range(base, base + GROUP)], axis=0
        )
        placed = jnp.dot(place, rows, preferred_element_type=jnp.float32)
        for i in range(GROUP):
            c = base + i
            mine = placed[i * CAP : (i + 1) * CAP]
            sent_ref[c, 0:CAP] = mine[:, 0:D].astype(jnp.bfloat16)
            used = slot < jnp.broadcast_to(count[c : c + 1], (CAP, D))
            sent_ref[c, CAP : 2 * CAP] = jnp.where(used, mine[:, D : 2 * D], EMPTY).astype(
                jnp.bfloat16
            )
            sent_ref[c, 2 * CAP : 3 * CAP] = mine[:, 2 * D : 3 * D].astype(jnp.bfloat16)


def pack(ids, q, k, v):
    return pl.pallas_call(
        pack_kernel,
        out_shape=(
            jax.ShapeDtypeStruct((CLUSTERS, 3 * CAP, D), jnp.bfloat16),
            jax.ShapeDtypeStruct((8, TOK), jnp.float32),
        ),
        in_specs=[VMEM] * 4,
        out_specs=(VMEM, VMEM),
        compiler_params=params(),
        name="pack_slots",
    )(ids, q, k, v)


def attend(queries, keys, values, allowed_of):
    scores = []
    for piece, allowed in zip(keys, allowed_of):
        s = lax.dot_general(
            queries, piece, (((1,), (1,)), ((), ())), preferred_element_type=jnp.float32
        )
        scores.append(s if allowed is None else jnp.where(allowed, s, NEVER))
    top = jnp.max(scores[0], axis=1, keepdims=True)
    for s in scores[1:]:
        top = jnp.maximum(top, jnp.max(s, axis=1, keepdims=True))
    shift = top * EXP_SCALE
    total = None
    for s, piece in zip(scores, values):
        weight = jnp.exp2(s * EXP_SCALE - shift).astype(jnp.bfloat16)
        part = jnp.dot(weight, piece, preferred_element_type=jnp.float32)
        total = part if total is None else total + part
    mass = total[:, D : 2 * D]
    return (total[:, 0:D] / jnp.where(mass > 0.0, mass, 1.0)).astype(jnp.bfloat16)


def routed_kernel(got_ref, out_ref, key_ref, value_ref):
    blocks = got_ref.shape[0]
    first = jnp.zeros((1, D), jnp.float32)
    for s in reversed(range(blocks)):
        row = got_ref[s, CAP : CAP + 16].astype(jnp.float32)[0:1]
        first = jnp.where(row < 100.0, row, first)
    filler = jnp.broadcast_to(first, (CAP, D))
    for s in range(blocks):
        key = got_ref[s, CAP : 2 * CAP].astype(jnp.float32)
        used = key < 100.0
        key_ref[s * CAP : (s + 1) * CAP] = jnp.where(used, key, filler).astype(jnp.bfloat16)
        value_ref[s * CAP : (s + 1) * CAP, 0:D] = got_ref[s, 2 * CAP : 3 * CAP]
        value_ref[s * CAP : (s + 1) * CAP, D : 2 * D] = used.astype(jnp.float32).astype(
            jnp.bfloat16
        )
    size = 2 * CAP
    within = lax.broadcasted_iota(jnp.int32, (size, size), 1) <= lax.broadcasted_iota(
        jnp.int32, (size, size), 0
    )
    for i in range(blocks // 2):
        low = i * size
        queries = got_ref[2 * i : 2 * i + 2, 0:CAP].reshape(size, D)
        keys, values, masks = [], [], []
        if low > 0:
            keys.append(key_ref[0:low])
            values.append(value_ref[0:low])
            masks.append(None)
        keys.append(key_ref[low : low + size])
        values.append(value_ref[low : low + size])
        masks.append(within)
        out_ref[2 * i : 2 * i + 2] = attend(queries, keys, values, masks).reshape(2, CAP, D)


def routed(got):
    blocks = got.shape[0]
    slots = blocks * CAP
    return pl.pallas_call(
        routed_kernel,
        out_shape=jax.ShapeDtypeStruct((blocks, CAP, D), jnp.bfloat16),
        in_specs=[VMEM],
        out_specs=VMEM,
        scratch_shapes=[
            pltpu.VMEM((slots, D), jnp.bfloat16),
            pltpu.VMEM((slots, 2 * D), jnp.bfloat16),
        ],
        compiler_params=params(),
        cost_estimate=pl.CostEstimate(
            flops=2 * slots * slots * D * 2, bytes_accessed=4 * slots * D * 2, transcendentals=0
        ),
        name="cluster_attention",
    )(got)


def local_kernel(at_ref, q_ref, k_ref, v_ref, far_ref, near_ref, out_ref, key_ref, value_ref):
    at = at_ref[0]
    own = k_ref[0:16].astype(jnp.float32)[0:1]
    nearest = near_ref[0, 0:16].astype(jnp.float32)[0:1]
    for b, ref in enumerate((far_ref, near_ref)):
        there = at >= 2 - b
        start = jnp.where(at == 0, own, nearest)
        filler = jnp.broadcast_to(start, (TOK, D))
        rows = pl.ds(b * TOK, TOK)
        key_ref[rows] = jnp.where(there, ref[0].astype(jnp.float32), filler).astype(jnp.bfloat16)
        value_ref[rows, 0:D] = ref[1]
        value_ref[rows, D : 2 * D] = jnp.full((TOK, D), jnp.where(there, 1.0, 0.0)).astype(
            jnp.bfloat16
        )
    key_ref[2 * TOK : 3 * TOK] = k_ref[...]
    value_ref[2 * TOK : 3 * TOK, 0:D] = v_ref[...]
    value_ref[2 * TOK : 3 * TOK, D : 2 * D] = jnp.ones((TOK, D), jnp.bfloat16)
    size = 256
    column = lax.broadcasted_iota(jnp.int32, (size, size), 1)
    line = lax.broadcasted_iota(jnp.int32, (size, size), 0)
    for i in range(TOK // size):
        low = i * size
        high = low + 2 * TOK
        spans = ((low, low + size), (low + size, high), (high, high + size))
        out_ref[low : low + size] = attend(
            q_ref[low : low + size],
            [key_ref[a:b] for a, b in spans],
            [value_ref[a:b] for a, b in spans],
            (column > line, None, column <= line),
        )


def windowed(at, q, k, v, far, near):
    return pl.pallas_call(
        local_kernel,
        out_shape=jax.ShapeDtypeStruct((TOK, D), jnp.bfloat16),
        in_specs=[pl.BlockSpec(memory_space=pltpu.SMEM)] + [VMEM] * 5,
        out_specs=VMEM,
        scratch_shapes=[
            pltpu.VMEM((3 * TOK, D), jnp.bfloat16),
            pltpu.VMEM((3 * TOK, 2 * D), jnp.bfloat16),
        ],
        compiler_params=params(),
        cost_estimate=pl.CostEstimate(
            flops=TOK * 2304 * D * 4, bytes_accessed=8 * TOK * D * 2, transcendentals=0
        ),
        name="window_attention",
    )(at, q, k, v, far, near)


def slot_kernel(ids_ref, rank_ref, at_rank_ref, ids_col_ref):
    rank = jnp.broadcast_to(rank_ref[0:1], (D, TOK)).T
    lane = lax.broadcasted_iota(jnp.int32, (TOK, CAP), 1)
    at_rank_ref[...] = (rank.astype(jnp.int32) == lane).astype(jnp.bfloat16)
    ids = jnp.broadcast_to(ids_ref[...].astype(jnp.float32), (D, TOK)).T
    ids_col_ref[...] = ids.astype(jnp.bfloat16)


def slots(ids, rank):
    return pl.pallas_call(
        slot_kernel,
        out_shape=(
            jax.ShapeDtypeStruct((TOK, CAP), jnp.bfloat16),
            jax.ShapeDtypeStruct((TOK, CAP), jnp.bfloat16),
        ),
        in_specs=[VMEM] * 2,
        out_specs=(VMEM, VMEM),
        compiler_params=params(),
        name="slot_columns",
    )(ids, rank)


def unpack_kernel(at_rank_ref, ids_ref, back_ref, out_ref):
    rows = 256
    for low in range(0, TOK, rows):
        at_rank = at_rank_ref[low : low + rows]
        ids = ids_ref[low : low + rows]
        zero = jnp.zeros_like(at_rank)
        picks = [
            jnp.where(ids == jnp.asarray(c, jnp.bfloat16), at_rank, zero) for c in range(CLUSTERS)
        ]
        pick = jnp.concatenate(picks, axis=1)
        out_ref[low : low + rows] = jnp.dot(
            pick, back_ref[...], preferred_element_type=jnp.float32
        ).astype(jnp.bfloat16)


def unpack(at_rank, ids_col, back):
    return pl.pallas_call(
        unpack_kernel,
        out_shape=jax.ShapeDtypeStruct((TOK, D), jnp.bfloat16),
        in_specs=[VMEM] * 3,
        out_specs=VMEM,
        compiler_params=params(),
        name="unpack_slots",
    )(at_rank, ids_col, back)


def passed_along(value, steps):
    count = lax.axis_size(SEQ)
    return lax.ppermute(value, SEQ, [(s, s + steps) for s in range(count - steps)])


def local(q_routed, k_routed, v_routed, memberships, q_local, k_local, v_local):
    seq_index = lax.axis_index(SEQ)
    pair = jnp.concatenate([k_local, v_local], axis=0)
    far = passed_along(pair, 2)
    near = passed_along(pair, 1)
    ids = memberships.reshape(1, TOK)
    sent, rank = pack(ids, q_routed[0], k_routed[0], v_routed[0])
    got = lax.all_to_all(sent, SEQ, split_axis=0, concat_axis=0, tiled=True)
    at_rank, ids_col = slots(ids, rank)
    out_local = windowed(
        seq_index.astype(jnp.int32).reshape(1), q_local[0], k_local[0], v_local[0], far, near
    )
    got, out_local = lax.optimization_barrier((got, out_local))
    mixed = routed(got)
    back = lax.all_to_all(mixed, SEQ, split_axis=0, concat_axis=0, tiled=True)
    out_routed = unpack(at_rank, ids_col, back.reshape(CLUSTERS * CAP, D))
    return (out_routed[None], out_local[None])


def solution(mesh):
    torus = Mesh(
        mesh.devices.reshape(mesh.shape["head"], 4, 4, 2), ("head", "seq_0", "seq_1", "seq_2")
    )
    spec = P("head", SEQ, None)
    return jax.shard_map(
        local,
        mesh=torus,
        in_specs=(spec,) * 7,
        out_specs=(spec, spec),
        check_vma=False,
    )
```

```python
import jax
import jax.numpy as jnp
from jax import lax
from jax.experimental import pallas as pl
from jax.experimental.pallas import tpu as pltpu
from jax.sharding import Mesh
from jax.sharding import PartitionSpec as P

CLUSTERS = 32
CAP = 128
TOK = 1024
D = 128
SEQ = ("seq_0", "seq_1", "seq_2")
LOG2E = 1.4426950408889634
EXP_SCALE = LOG2E * D**-0.5
NEVER = -1e30
EMPTY = 256.0
GROUP = 8
CHUNK = 1024
VMEM = pl.BlockSpec(memory_space=pltpu.VMEM)


def params():
    return pltpu.CompilerParams(vmem_limit_bytes=56 * 1024 * 1024)


def pack_kernel(ids_ref, q_ref, k_ref, v_ref, sent_ref, rank_ref):
    ids = ids_ref[...]
    member = (ids == lax.broadcasted_iota(jnp.int32, (CLUSTERS, TOK), 0)).astype(jnp.float32)
    member_b = member.astype(jnp.bfloat16)
    upto = (
        lax.broadcasted_iota(jnp.int32, (128, 128), 0)
        <= lax.broadcasted_iota(jnp.int32, (128, 128), 1)
    ).astype(jnp.bfloat16)
    count = jnp.zeros((CLUSTERS, 1), jnp.float32)
    ranks = []
    for first in range(0, TOK, 128):
        seen = count + jnp.dot(
            member_b[:, first : first + 128], upto, preferred_element_type=jnp.float32
        )
        ranks.append(
            jnp.sum(member[:, first : first + 128] * seen, axis=0, keepdims=True) - 1.0
        )
        count = seen[:, 127:128]
    rank = jnp.concatenate(ranks, axis=1)
    rank_ref[...] = jnp.broadcast_to(rank, rank_ref.shape)
    at_rank = (
        rank.astype(jnp.int32) == lax.broadcasted_iota(jnp.int32, (CAP, TOK), 0)
    ).astype(jnp.bfloat16)
    rows = jnp.concatenate([q_ref[...], k_ref[...], v_ref[...]], axis=1)
    slot = lax.broadcasted_iota(jnp.int32, (CAP, D), 0).astype(jnp.float32)
    for base in range(0, CLUSTERS, GROUP):
        place = jnp.concatenate(
            [at_rank * member_b[c : c + 1] for c in range(base, base + GROUP)], axis=0
        )
        placed = jnp.dot(place, rows, preferred_element_type=jnp.float32)
        for i in range(GROUP):
            c = base + i
            mine = placed[i * CAP : (i + 1) * CAP]
            sent_ref[c, 0:CAP] = mine[:, 0:D].astype(jnp.bfloat16)
            used = slot < jnp.broadcast_to(count[c : c + 1], (CAP, D))
            sent_ref[c, CAP : 2 * CAP] = jnp.where(used, mine[:, D : 2 * D], EMPTY).astype(
                jnp.bfloat16
            )
            sent_ref[c, 2 * CAP : 3 * CAP] = mine[:, 2 * D : 3 * D].astype(jnp.bfloat16)


def pack(ids, q, k, v):
    return pl.pallas_call(
        pack_kernel,
        out_shape=(
            jax.ShapeDtypeStruct((CLUSTERS, 3 * CAP, D), jnp.bfloat16),
            jax.ShapeDtypeStruct((8, TOK), jnp.float32),
        ),
        in_specs=[VMEM] * 4,
        out_specs=(VMEM, VMEM),
        compiler_params=params(),
        name="pack_slots",
    )(ids, q, k, v)


def attend(tasks, query_of, key_ref, value_ref, write):
    def score(task):
        block, low, high, mask, _, _ = task
        s = lax.dot_general(
            query_of(block),
            key_ref[low:high],
            (((1,), (1,)), ((), ())),
            preferred_element_type=jnp.float32,
        )
        return s if mask is None else jnp.where(mask, s, NEVER)

    coming = score(tasks[0])
    for t, (block, low, high, _, first, last) in enumerate(tasks):
        s = coming
        if t + 1 < len(tasks):
            coming = score(tasks[t + 1])
        top = jnp.max(s, axis=1, keepdims=True)
        if not first:
            top = jnp.maximum(top, top_before)
        weight = jnp.exp2(s * EXP_SCALE - top * EXP_SCALE).astype(jnp.bfloat16)
        total = jnp.dot(weight, value_ref[low:high], preferred_element_type=jnp.float32)
        if not first:
            total = total + total_before * jnp.exp2((top_before - top) * EXP_SCALE)
        top_before, total_before = top, total
        if last:
            mass = total[:, D : 2 * D]
            write(
                block, (total[:, 0:D] / jnp.where(mass > 0.0, mass, 1.0)).astype(jnp.bfloat16)
            )


def tasks_of(block, spans):
    return [
        (block, low, high, mask, t == 0, t == len(spans) - 1)
        for t, (low, high, mask) in enumerate(spans)
    ]


def routed_kernel(got_ref, out_ref, key_ref, value_ref):
    blocks = got_ref.shape[0]
    first = jnp.zeros((1, D), jnp.float32)
    for s in reversed(range(blocks)):
        row = got_ref[s, CAP : CAP + 16].astype(jnp.float32)[0:1]
        first = jnp.where(row < 100.0, row, first)
    filler = jnp.broadcast_to(first, (CAP, D))
    for s in range(blocks):
        key = got_ref[s, CAP : 2 * CAP].astype(jnp.float32)
        used = key < 100.0
        key_ref[s * CAP : (s + 1) * CAP] = jnp.where(used, key, filler).astype(jnp.bfloat16)
        value_ref[s * CAP : (s + 1) * CAP, 0:D] = got_ref[s, 2 * CAP : 3 * CAP]
        value_ref[s * CAP : (s + 1) * CAP, D : 2 * D] = used.astype(jnp.float32).astype(
            jnp.bfloat16
        )
    size = 2 * CAP
    within = lax.broadcasted_iota(jnp.int32, (size, size), 1) <= lax.broadcasted_iota(
        jnp.int32, (size, size), 0
    )
    tasks = []
    for i in range(blocks // 2):
        own = i * size
        spans = [(low, min(low + CHUNK, own), None) for low in range(0, own, CHUNK)]
        tasks += tasks_of(i, spans + [(own, own + size, within)])

    def write(i, mixed):
        out_ref[2 * i : 2 * i + 2] = mixed.reshape(2, CAP, D)

    attend(
        tasks,
        lambda i: got_ref[2 * i : 2 * i + 2, 0:CAP].reshape(size, D),
        key_ref,
        value_ref,
        write,
    )


def routed(got):
    blocks = got.shape[0]
    slots = blocks * CAP
    return pl.pallas_call(
        routed_kernel,
        out_shape=jax.ShapeDtypeStruct((blocks, CAP, D), jnp.bfloat16),
        in_specs=[VMEM],
        out_specs=VMEM,
        scratch_shapes=[
            pltpu.VMEM((slots, D), jnp.bfloat16),
            pltpu.VMEM((slots, 2 * D), jnp.bfloat16),
        ],
        compiler_params=params(),
        cost_estimate=pl.CostEstimate(
            flops=2 * slots * slots * D * 2, bytes_accessed=4 * slots * D * 2, transcendentals=0
        ),
        name="cluster_attention",
    )(got)


def local_kernel(
    at_ref, q_ref, k_ref, v_ref, far_k_ref, far_v_ref, near_ref, out_ref, key_ref, value_ref
):
    at = at_ref[0]
    own = k_ref[0:16].astype(jnp.float32)[0:1]
    nearest = near_ref[0, 0:16].astype(jnp.float32)[0:1]
    earlier = ((far_k_ref[...], far_v_ref[...]), (near_ref[0], near_ref[1]))
    for b, (key, value) in enumerate(earlier):
        there = at >= 2 - b
        start = jnp.where(at == 0, own, nearest)
        filler = jnp.broadcast_to(start, (TOK, D))
        rows = pl.ds(b * TOK, TOK)
        key_ref[rows] = jnp.where(there, key.astype(jnp.float32), filler).astype(jnp.bfloat16)
        value_ref[rows, 0:D] = value
        value_ref[rows, D : 2 * D] = jnp.full((TOK, D), jnp.where(there, 1.0, 0.0)).astype(
            jnp.bfloat16
        )
    key_ref[2 * TOK : 3 * TOK] = k_ref[...]
    value_ref[2 * TOK : 3 * TOK, 0:D] = v_ref[...]
    value_ref[2 * TOK : 3 * TOK, D : 2 * D] = jnp.ones((TOK, D), jnp.bfloat16)
    size = 256
    column = lax.broadcasted_iota(jnp.int32, (size, size), 1)
    line = lax.broadcasted_iota(jnp.int32, (size, size), 0)
    tasks = []
    for i in range(TOK // size):
        low = i * size
        high = low + 2 * TOK
        middle = low + size + CHUNK
        spans = [
            (low, low + size, column > line),
            (low + size, middle, None),
            (middle, high, None),
            (high, high + size, column <= line),
        ]
        tasks += tasks_of(i, spans)

    def write(i, mixed):
        out_ref[i * size : (i + 1) * size] = mixed

    attend(
        tasks, lambda i: q_ref[i * size : (i + 1) * size], key_ref, value_ref, write
    )


def windowed(at, q, k, v, far_k, far_v, near):
    return pl.pallas_call(
        local_kernel,
        out_shape=jax.ShapeDtypeStruct((TOK, D), jnp.bfloat16),
        in_specs=[pl.BlockSpec(memory_space=pltpu.SMEM)] + [VMEM] * 6,
        out_specs=VMEM,
        scratch_shapes=[
            pltpu.VMEM((3 * TOK, D), jnp.bfloat16),
            pltpu.VMEM((3 * TOK, 2 * D), jnp.bfloat16),
        ],
        compiler_params=params(),
        cost_estimate=pl.CostEstimate(
            flops=TOK * 2304 * D * 4, bytes_accessed=8 * TOK * D * 2, transcendentals=0
        ),
        name="window_attention",
    )(at, q, k, v, far_k, far_v, near)


def slot_kernel(ids_ref, rank_ref, at_rank_ref, ids_col_ref):
    rank = jnp.broadcast_to(rank_ref[0:1], (D, TOK)).T
    lane = lax.broadcasted_iota(jnp.int32, (TOK, CAP), 1)
    at_rank_ref[...] = (rank.astype(jnp.int32) == lane).astype(jnp.bfloat16)
    ids = jnp.broadcast_to(ids_ref[...].astype(jnp.float32), (D, TOK)).T
    ids_col_ref[...] = ids.astype(jnp.bfloat16)


def slots(ids, rank):
    return pl.pallas_call(
        slot_kernel,
        out_shape=(
            jax.ShapeDtypeStruct((TOK, CAP), jnp.bfloat16),
            jax.ShapeDtypeStruct((TOK, CAP), jnp.bfloat16),
        ),
        in_specs=[VMEM] * 2,
        out_specs=(VMEM, VMEM),
        compiler_params=params(),
        name="slot_columns",
    )(ids, rank)


def unpack_kernel(at_rank_ref, ids_ref, back_ref, out_ref):
    rows = 256
    for low in range(0, TOK, rows):
        at_rank = at_rank_ref[low : low + rows]
        ids = ids_ref[low : low + rows]
        zero = jnp.zeros_like(at_rank)
        picks = [
            jnp.where(ids == jnp.asarray(c, jnp.bfloat16), at_rank, zero) for c in range(CLUSTERS)
        ]
        pick = jnp.concatenate(picks, axis=1)
        out_ref[low : low + rows] = jnp.dot(
            pick, back_ref[...], preferred_element_type=jnp.float32
        ).astype(jnp.bfloat16)


def unpack(at_rank, ids_col, back):
    return pl.pallas_call(
        unpack_kernel,
        out_shape=jax.ShapeDtypeStruct((TOK, D), jnp.bfloat16),
        in_specs=[VMEM] * 3,
        out_specs=VMEM,
        compiler_params=params(),
        name="unpack_slots",
    )(at_rank, ids_col, back)


def passed_along(value, steps):
    count = lax.axis_size(SEQ)
    return lax.ppermute(value, SEQ, [(s, s + steps) for s in range(count - steps)])


def local(q_routed, k_routed, v_routed, memberships, q_local, k_local, v_local):
    seq_index = lax.axis_index(SEQ)
    far_k = passed_along(k_local, 2)
    far_v = passed_along(v_local, 2)
    ids = memberships.reshape(1, TOK)
    sent, rank = pack(ids, q_routed[0], k_routed[0], v_routed[0])
    sent, far_k, far_v = lax.optimization_barrier((sent, far_k, far_v))
    given = jnp.where(
        seq_index % 2 == 1,
        jnp.concatenate([far_k, far_v], axis=0),
        jnp.concatenate([k_local, v_local], axis=0),
    )
    near = lax.ppermute(given, SEQ, [(s, s ^ 1) for s in range(lax.axis_size(SEQ))])
    got = lax.all_to_all(sent, SEQ, split_axis=0, concat_axis=0, tiled=True)
    at_rank, ids_col = slots(ids, rank)
    out_local = windowed(
        seq_index.astype(jnp.int32).reshape(1), q_local[0], k_local[0], v_local[0], far_k[0], far_v[0], near
    )
    got, out_local = lax.optimization_barrier((got, out_local))
    mixed = routed(got)
    back = lax.all_to_all(mixed, SEQ, split_axis=0, concat_axis=0, tiled=True)
    out_routed = unpack(at_rank, ids_col, back.reshape(CLUSTERS * CAP, D))
    return (out_routed[None], out_local[None])


def solution(mesh):
    torus = Mesh(
        mesh.devices.reshape(mesh.shape["head"], 4, 4, 2), ("head", "seq_0", "seq_1", "seq_2")
    )
    spec = P("head", SEQ, None)
    return jax.shard_map(
        local,
        mesh=torus,
        in_specs=(spec,) * 7,
        out_specs=(spec, spec),
        check_vma=False,
    )
```

```python
import jax
import jax.numpy as jnp
from jax import lax
from jax.experimental import pallas as pl
from jax.experimental.pallas import tpu as pltpu
from jax.sharding import Mesh
from jax.sharding import PartitionSpec as P

CLUSTERS = 32
CAP = 128
TOK = 1024
D = 128
SEQ = ("seq_0", "seq_1", "seq_2")
LOG2E = 1.4426950408889634
EXP_SCALE = LOG2E * D**-0.5
NEVER = -1e30
EMPTY = 256.0
GROUP = 8
CHUNK = 1024
VMEM = pl.BlockSpec(memory_space=pltpu.VMEM)


def in_vmem(array):
    return pltpu.with_memory_space_constraint(array, pltpu.VMEM)


def params():
    return pltpu.CompilerParams(vmem_limit_bytes=40 * 1024 * 1024)


def pack_kernel(ids_ref, q_ref, k_ref, v_ref, sent_ref, rank_ref):
    ids = ids_ref[...]
    member = (ids == lax.broadcasted_iota(jnp.int32, (CLUSTERS, TOK), 0)).astype(jnp.float32)
    member_b = member.astype(jnp.bfloat16)
    upto = (
        lax.broadcasted_iota(jnp.int32, (128, 128), 0)
        <= lax.broadcasted_iota(jnp.int32, (128, 128), 1)
    ).astype(jnp.bfloat16)
    count = jnp.zeros((CLUSTERS, 1), jnp.float32)
    ranks = []
    for first in range(0, TOK, 128):
        seen = count + jnp.dot(
            member_b[:, first : first + 128], upto, preferred_element_type=jnp.float32
        )
        ranks.append(
            jnp.sum(member[:, first : first + 128] * seen, axis=0, keepdims=True) - 1.0
        )
        count = seen[:, 127:128]
    rank = jnp.concatenate(ranks, axis=1)
    rank_ref[...] = jnp.broadcast_to(rank, rank_ref.shape)
    at_rank = (
        rank.astype(jnp.int32) == lax.broadcasted_iota(jnp.int32, (CAP, TOK), 0)
    ).astype(jnp.bfloat16)
    rows = jnp.concatenate([q_ref[...], k_ref[...], v_ref[...]], axis=1)
    slot = lax.broadcasted_iota(jnp.int32, (CAP, D), 0).astype(jnp.float32)
    for base in range(0, CLUSTERS, GROUP):
        place = jnp.concatenate(
            [at_rank * member_b[c : c + 1] for c in range(base, base + GROUP)], axis=0
        )
        placed = jnp.dot(place, rows, preferred_element_type=jnp.float32)
        for i in range(GROUP):
            c = base + i
            mine = placed[i * CAP : (i + 1) * CAP]
            sent_ref[c, 0:CAP] = mine[:, 0:D].astype(jnp.bfloat16)
            used = slot < jnp.broadcast_to(count[c : c + 1], (CAP, D))
            sent_ref[c, CAP : 2 * CAP] = jnp.where(used, mine[:, D : 2 * D], EMPTY).astype(
                jnp.bfloat16
            )
            sent_ref[c, 2 * CAP : 3 * CAP] = mine[:, 2 * D : 3 * D].astype(jnp.bfloat16)


def pack(ids, q, k, v):
    return pl.pallas_call(
        pack_kernel,
        out_shape=(
            jax.ShapeDtypeStruct((CLUSTERS, 3 * CAP, D), jnp.bfloat16),
            pltpu.VMEM((8, TOK), jnp.float32),
        ),
        in_specs=[VMEM] * 4,
        out_specs=(VMEM, VMEM),
        compiler_params=params(),
        name="pack_slots",
    )(ids, q, k, v)


def attend(tasks, query_of, key_ref, value_ref, write):
    def score(task):
        block, low, high, mask, _, _ = task
        s = lax.dot_general(
            query_of(block),
            key_ref[low:high],
            (((1,), (1,)), ((), ())),
            preferred_element_type=jnp.float32,
        )
        return s if mask is None else jnp.where(mask, s, NEVER)

    coming = score(tasks[0])
    for t, (block, low, high, _, first, last) in enumerate(tasks):
        s = coming
        if t + 1 < len(tasks):
            coming = score(tasks[t + 1])
        top = jnp.max(s, axis=1, keepdims=True)
        if not first:
            top = jnp.maximum(top, top_before)
        weight = jnp.exp2(s * EXP_SCALE - top * EXP_SCALE).astype(jnp.bfloat16)
        total = jnp.dot(weight, value_ref[low:high], preferred_element_type=jnp.float32)
        if not first:
            total = total + total_before * jnp.exp2((top_before - top) * EXP_SCALE)
        top_before, total_before = top, total
        if last:
            mass = total[:, D : 2 * D]
            write(
                block, (total[:, 0:D] / jnp.where(mass > 0.0, mass, 1.0)).astype(jnp.bfloat16)
            )


def tasks_of(block, spans):
    return [
        (block, low, high, mask, t == 0, t == len(spans) - 1)
        for t, (low, high, mask) in enumerate(spans)
    ]


def routed_kernel(got_ref, out_ref, key_ref, value_ref):
    blocks = got_ref.shape[0]
    first = jnp.zeros((1, D), jnp.float32)
    for s in reversed(range(blocks)):
        row = got_ref[s, CAP : CAP + 16].astype(jnp.float32)[0:1]
        first = jnp.where(row < 100.0, row, first)
    filler = jnp.broadcast_to(first, (CAP, D))
    for s in range(blocks):
        key = got_ref[s, CAP : 2 * CAP].astype(jnp.float32)
        used = key < 100.0
        key_ref[s * CAP : (s + 1) * CAP] = jnp.where(used, key, filler).astype(jnp.bfloat16)
        value_ref[s * CAP : (s + 1) * CAP, 0:D] = got_ref[s, 2 * CAP : 3 * CAP]
        value_ref[s * CAP : (s + 1) * CAP, D : 2 * D] = used.astype(jnp.float32).astype(
            jnp.bfloat16
        )
    size = 2 * CAP
    within = lax.broadcasted_iota(jnp.int32, (size, size), 1) <= lax.broadcasted_iota(
        jnp.int32, (size, size), 0
    )
    tasks = []
    for i in range(blocks // 2):
        own = i * size
        spans = [(low, min(low + CHUNK, own), None) for low in range(0, own, CHUNK)]
        tasks += tasks_of(i, spans + [(own, own + size, within)])

    def write(i, mixed):
        out_ref[2 * i : 2 * i + 2] = mixed.reshape(2, CAP, D)

    attend(
        tasks,
        lambda i: got_ref[2 * i : 2 * i + 2, 0:CAP].reshape(size, D),
        key_ref,
        value_ref,
        write,
    )


def routed(got):
    blocks = got.shape[0]
    slots = blocks * CAP
    return pl.pallas_call(
        routed_kernel,
        out_shape=jax.ShapeDtypeStruct((blocks, CAP, D), jnp.bfloat16),
        in_specs=[VMEM],
        out_specs=VMEM,
        scratch_shapes=[
            pltpu.VMEM((slots, D), jnp.bfloat16),
            pltpu.VMEM((slots, 2 * D), jnp.bfloat16),
        ],
        compiler_params=params(),
        cost_estimate=pl.CostEstimate(
            flops=2 * slots * slots * D * 2, bytes_accessed=4 * slots * D * 2, transcendentals=0
        ),
        name="cluster_attention",
    )(in_vmem(got))


def local_kernel(
    at_ref, q_ref, k_ref, v_ref, far_ref, near_ref, out_ref, key_ref, value_ref
):
    at = at_ref[0]
    own = k_ref[0:16].astype(jnp.float32)[0:1]
    nearest = near_ref[0, 0:16].astype(jnp.float32)[0:1]
    earlier = ((far_ref[0], far_ref[1]), (near_ref[0], near_ref[1]))
    for b, (key, value) in enumerate(earlier):
        there = at >= 2 - b
        start = jnp.where(at == 0, own, nearest)
        filler = jnp.broadcast_to(start, (TOK, D))
        rows = pl.ds(b * TOK, TOK)
        key_ref[rows] = jnp.where(there, key.astype(jnp.float32), filler).astype(jnp.bfloat16)
        value_ref[rows, 0:D] = value
        value_ref[rows, D : 2 * D] = jnp.full((TOK, D), jnp.where(there, 1.0, 0.0)).astype(
            jnp.bfloat16
        )
    key_ref[2 * TOK : 3 * TOK] = k_ref[...]
    value_ref[2 * TOK : 3 * TOK, 0:D] = v_ref[...]
    value_ref[2 * TOK : 3 * TOK, D : 2 * D] = jnp.ones((TOK, D), jnp.bfloat16)
    size = 256
    column = lax.broadcasted_iota(jnp.int32, (size, size), 1)
    line = lax.broadcasted_iota(jnp.int32, (size, size), 0)
    tasks = []
    for i in range(TOK // size):
        low = i * size
        high = low + 2 * TOK
        middle = low + size + CHUNK
        spans = [
            (low, low + size, column > line),
            (low + size, middle, None),
            (middle, high, None),
            (high, high + size, column <= line),
        ]
        tasks += tasks_of(i, spans)

    def write(i, mixed):
        out_ref[i * size : (i + 1) * size] = mixed

    attend(
        tasks, lambda i: q_ref[i * size : (i + 1) * size], key_ref, value_ref, write
    )


def windowed(at, q, k, v, far, near):
    return pl.pallas_call(
        local_kernel,
        out_shape=jax.ShapeDtypeStruct((TOK, D), jnp.bfloat16),
        in_specs=[pl.BlockSpec(memory_space=pltpu.SMEM)] + [VMEM] * 5,
        out_specs=VMEM,
        scratch_shapes=[
            pltpu.VMEM((3 * TOK, D), jnp.bfloat16),
            pltpu.VMEM((3 * TOK, 2 * D), jnp.bfloat16),
        ],
        compiler_params=params(),
        cost_estimate=pl.CostEstimate(
            flops=TOK * 2304 * D * 4, bytes_accessed=8 * TOK * D * 2, transcendentals=0
        ),
        name="window_attention",
    )(at, q, k, v, in_vmem(far), in_vmem(near))


def slot_kernel(ids_ref, rank_ref, at_rank_ref, ids_col_ref):
    rank = jnp.broadcast_to(rank_ref[0:1], (D, TOK)).T
    lane = lax.broadcasted_iota(jnp.int32, (TOK, CAP), 1)
    at_rank_ref[...] = (rank.astype(jnp.int32) == lane).astype(jnp.bfloat16)
    ids = jnp.broadcast_to(ids_ref[...].astype(jnp.float32), (D, TOK)).T
    ids_col_ref[...] = ids.astype(jnp.bfloat16)


def slots(ids, rank):
    return pl.pallas_call(
        slot_kernel,
        out_shape=(
            pltpu.VMEM((TOK, CAP), jnp.bfloat16),
            pltpu.VMEM((TOK, CAP), jnp.bfloat16),
        ),
        in_specs=[VMEM] * 2,
        out_specs=(VMEM, VMEM),
        compiler_params=params(),
        name="slot_columns",
    )(ids, in_vmem(rank))


def unpack_kernel(at_rank_ref, ids_ref, back_ref, out_ref):
    rows = 256
    for low in range(0, TOK, rows):
        at_rank = at_rank_ref[low : low + rows]
        ids = ids_ref[low : low + rows]
        zero = jnp.zeros_like(at_rank)
        picks = [
            jnp.where(ids == jnp.asarray(c, jnp.bfloat16), at_rank, zero) for c in range(CLUSTERS)
        ]
        pick = jnp.concatenate(picks, axis=1)
        out_ref[low : low + rows] = jnp.dot(
            pick, back_ref[...], preferred_element_type=jnp.float32
        ).astype(jnp.bfloat16)


def unpack(at_rank, ids_col, back):
    return pl.pallas_call(
        unpack_kernel,
        out_shape=jax.ShapeDtypeStruct((TOK, D), jnp.bfloat16),
        in_specs=[VMEM] * 3,
        out_specs=VMEM,
        compiler_params=params(),
        name="unpack_slots",
    )(in_vmem(at_rank), in_vmem(ids_col), in_vmem(back))


def passed_along(value, steps):
    count = lax.axis_size(SEQ)
    return lax.ppermute(value, SEQ, [(s, s + steps) for s in range(count - steps)])


def local(q_routed, k_routed, v_routed, memberships, q_local, k_local, v_local):
    seq_index = lax.axis_index(SEQ)
    ids = memberships.reshape(1, TOK)
    sent, rank = pack(ids, q_routed[0], k_routed[0], v_routed[0])
    got = lax.all_to_all(sent, SEQ, split_axis=0, concat_axis=0, tiled=True)
    pair = jnp.concatenate([k_local, v_local], axis=0)
    at_rank, ids_col = slots(ids, rank)
    got, pair, at_rank, ids_col = lax.optimization_barrier((got, pair, at_rank, ids_col))
    far = passed_along(pair, 2)
    mixed = routed(got)
    mixed, far = lax.optimization_barrier((mixed, far))
    back = lax.all_to_all(mixed, SEQ, split_axis=0, concat_axis=0, tiled=True)
    given = jnp.where(seq_index % 2 == 1, far, pair)
    near = lax.ppermute(given, SEQ, [(s, s ^ 1) for s in range(lax.axis_size(SEQ))])
    out_local = windowed(
        seq_index.astype(jnp.int32).reshape(1), q_local[0], k_local[0], v_local[0], far, near
    )
    back, out_local = lax.optimization_barrier((back, out_local))
    out_routed = unpack(at_rank, ids_col, back.reshape(CLUSTERS * CAP, D))
    return (out_routed[None], out_local[None])


def solution(mesh):
    torus = Mesh(
        mesh.devices.reshape(mesh.shape["head"], 4, 4, 2), ("head", "seq_0", "seq_1", "seq_2")
    )
    spec = P("head", SEQ, None)
    return jax.shard_map(
        local,
        mesh=torus,
        in_specs=(spec,) * 7,
        out_specs=(spec, spec),
        check_vma=False,
    )
```

```python
import jax
import jax.numpy as jnp
from jax import lax
from jax.experimental import pallas as pl
from jax.experimental.pallas import tpu as pltpu
from jax.sharding import Mesh
from jax.sharding import PartitionSpec as P

CLUSTERS = 32
CAP = 128
TOK = 1024
D = 128
SEQ = ("seq_0", "seq_1", "seq_2")
LOG2E = 1.4426950408889634
EXP_SCALE = LOG2E * D**-0.5
NEVER = -1e30
EMPTY = 256.0
GROUP = 8
CHUNK = 1024
SENDS = (0, 24, 32)
VMEM = pl.BlockSpec(memory_space=pltpu.VMEM)
HBM = pl.BlockSpec(memory_space=pltpu.HBM)


def in_vmem(array):
    return pltpu.with_memory_space_constraint(array, pltpu.VMEM)


def in_hbm(array):
    return pltpu.with_memory_space_constraint(array, pltpu.HBM)


def params():
    return pltpu.CompilerParams(vmem_limit_bytes=40 * 1024 * 1024)


def pack_kernel(
    ids_ref,
    q_ref,
    k_ref,
    v_ref,
    sent_ref,
    place_ref,
    start_ref,
    rows_ref,
    sorted_ref,
    stage_ref,
    start_smem,
    in_sems,
    out_sems,
    start_sem,
):
    loads = [
        pltpu.make_async_copy(ref, rows_ref.at[i], in_sems.at[i])
        for i, ref in enumerate((q_ref, k_ref, v_ref))
    ]
    for load in loads:
        load.start()
    ids = ids_ref[...]
    cluster = lax.broadcasted_iota(jnp.int32, (CLUSTERS, TOK), 0)
    member = (ids == cluster).astype(jnp.float32)
    member_b = member.astype(jnp.bfloat16)
    upto = (
        lax.broadcasted_iota(jnp.int32, (128, 128), 0)
        <= lax.broadcasted_iota(jnp.int32, (128, 128), 1)
    ).astype(jnp.bfloat16)
    count = jnp.zeros((CLUSTERS, 1), jnp.float32)
    ranks = []
    for first in range(0, TOK, 128):
        seen = count + jnp.dot(
            member_b[:, first : first + 128], upto, preferred_element_type=jnp.float32
        )
        ranks.append(
            jnp.sum(member[:, first : first + 128] * seen, axis=0, keepdims=True) - 1.0
        )
        count = seen[:, 127:128]
    line = lax.broadcasted_iota(jnp.int32, (CLUSTERS, 128), 0)
    lane = lax.broadcasted_iota(jnp.int32, (CLUSTERS, 128), 1)
    start = jnp.sum(
        jnp.where(line < lane, jnp.broadcast_to(count, (CLUSTERS, 128)), 0.0),
        axis=0,
        keepdims=True,
    )
    start_ref[...] = jnp.broadcast_to(start, start_ref.shape).astype(jnp.int32)
    starts = pltpu.make_async_copy(start_ref, start_smem, start_sem)
    starts.start()
    before = jnp.sum(
        jnp.where(cluster < ids, jnp.broadcast_to(count, (CLUSTERS, TOK)), 0.0),
        axis=0,
        keepdims=True,
    )
    place = before + jnp.concatenate(ranks, axis=1)
    place_ref[...] = jnp.broadcast_to(place, place_ref.shape)
    place = place.astype(jnp.int32)
    for load in loads:
        load.wait()
    rows = jnp.concatenate([rows_ref[i] for i in range(3)], axis=1)
    size = 256
    for low in range(0, TOK, size):
        line = lax.broadcasted_iota(jnp.int32, (size, TOK), 0) + low
        in_order = jnp.dot(
            (place == line).astype(jnp.float32).astype(jnp.bfloat16),
            rows,
            preferred_element_type=jnp.float32,
        )
        for i in range(3):
            sorted_ref[i, low : low + size] = in_order[:, i * D : (i + 1) * D]
    starts.wait()
    slot = lax.broadcasted_iota(jnp.int32, (CAP, D), 0)
    sends = []
    for base in range(0, CLUSTERS, GROUP):
        for c in range(base, base + GROUP):
            first = start_smem[0, c]
            used = slot < start_smem[0, c + 1] - first
            for i, blank in enumerate((0.0, EMPTY, 0.0)):
                mine = jnp.where(used, sorted_ref[i, pl.ds(first, CAP)], blank)
                stage_ref[c, i * CAP : (i + 1) * CAP] = mine.astype(jnp.bfloat16)
        part = pl.ds(base, GROUP)
        sends.append(
            pltpu.make_async_copy(
                stage_ref.at[part], sent_ref.at[part], out_sems.at[base // GROUP]
            )
        )
        sends[-1].start()
    for send in sends:
        send.wait()


def pack(ids, q, k, v):
    return pl.pallas_call(
        pack_kernel,
        out_shape=(
            pltpu.HBM((CLUSTERS, 3 * CAP, D), jnp.bfloat16),
            pltpu.VMEM((8, TOK), jnp.float32),
            pltpu.VMEM((8, 128), jnp.int32),
        ),
        in_specs=[VMEM] + [HBM] * 3,
        out_specs=(HBM, VMEM, VMEM),
        scratch_shapes=[
            pltpu.VMEM((3, TOK, D), jnp.bfloat16),
            pltpu.VMEM((3, TOK + CAP, D), jnp.float32),
            pltpu.VMEM((CLUSTERS, 3 * CAP, D), jnp.bfloat16),
            pltpu.SMEM((8, 128), jnp.int32),
            pltpu.SemaphoreType.DMA((3,)),
            pltpu.SemaphoreType.DMA((CLUSTERS // GROUP,)),
            pltpu.SemaphoreType.DMA,
        ],
        compiler_params=params(),
        name="pack_slots",
    )(ids, in_hbm(q), in_hbm(k), in_hbm(v))


def attend(tasks, query_of, key_ref, value_ref, write):
    def score(task):
        block, low, high, mask, _, _ = task
        s = lax.dot_general(
            query_of(block),
            key_ref[low:high],
            (((1,), (1,)), ((), ())),
            preferred_element_type=jnp.float32,
        )
        return s if mask is None else jnp.where(mask, s, NEVER)

    coming = score(tasks[0])
    for t, (block, low, high, _, first, last) in enumerate(tasks):
        s = coming
        if t + 1 < len(tasks):
            coming = score(tasks[t + 1])
        top = jnp.max(s, axis=1, keepdims=True)
        if not first:
            top = jnp.maximum(top, top_before)
        weight = jnp.exp2(s * EXP_SCALE - top * EXP_SCALE).astype(jnp.bfloat16)
        total = jnp.dot(weight, value_ref[low:high], preferred_element_type=jnp.float32)
        if not first:
            total = total + total_before * jnp.exp2((top_before - top) * EXP_SCALE)
        top_before, total_before = top, total
        if last:
            mass = total[:, D : 2 * D]
            write(
                block, (total[:, 0:D] / jnp.where(mass > 0.0, mass, 1.0)).astype(jnp.bfloat16)
            )


def tasks_of(block, spans):
    return [
        (block, low, high, mask, t == 0, t == len(spans) - 1)
        for t, (low, high, mask) in enumerate(spans)
    ]


def routed_kernel(
    got_ref,
    out_ref,
    key_ref,
    value_ref,
    mixed_ref,
    out_sems,
):
    blocks = got_ref.shape[0]
    first = jnp.zeros((1, D), jnp.float32)
    for s in reversed(range(blocks)):
        row = got_ref[s, CAP : CAP + 16].astype(jnp.float32)[0:1]
        first = jnp.where(row < 100.0, row, first)
    filler = jnp.broadcast_to(first, (CAP, D))
    size = 2 * CAP
    within = lax.broadcasted_iota(jnp.int32, (size, size), 1) <= lax.broadcasted_iota(
        jnp.int32, (size, size), 0
    )
    for s in range(blocks):
        at = slice(s * CAP, (s + 1) * CAP)
        key = got_ref[s, CAP : 2 * CAP].astype(jnp.float32)
        used = key < 100.0
        key_ref[at] = jnp.where(used, key, filler).astype(jnp.bfloat16)
        value_ref[at, 0:D] = got_ref[s, 2 * CAP : 3 * CAP]
        value_ref[at, D : 2 * D] = used.astype(jnp.float32).astype(jnp.bfloat16)

    def query_of(i):
        return got_ref[2 * i : 2 * i + 2, 0:CAP].reshape(size, D)

    tasks = []
    for i in range(blocks // 2):
        own = i * size
        spans = [(low, min(low + CHUNK, own), None) for low in range(0, own, CHUNK)]
        tasks += tasks_of(i, spans + [(own, own + size, within)])
    sends = []

    def write(i, mixed):
        mixed_ref[2 * i : 2 * i + 2] = mixed.reshape(2, CAP, D)
        if 2 * i + 2 in SENDS:
            n = SENDS.index(2 * i + 2)
            part = pl.ds(SENDS[n - 1], SENDS[n] - SENDS[n - 1])
            sends.append(
                pltpu.make_async_copy(mixed_ref.at[part], out_ref.at[part], out_sems.at[n - 1])
            )
            sends[-1].start()

    attend(tasks, query_of, key_ref, value_ref, write)
    for send in sends:
        send.wait()


def routed(got):
    blocks = got.shape[0]
    slots = blocks * CAP
    return pl.pallas_call(
        routed_kernel,
        out_shape=pltpu.HBM((blocks, CAP, D), jnp.bfloat16),
        in_specs=[VMEM],
        out_specs=HBM,
        scratch_shapes=[
            pltpu.VMEM((slots, D), jnp.bfloat16),
            pltpu.VMEM((slots, 2 * D), jnp.bfloat16),
            pltpu.VMEM((blocks, CAP, D), jnp.bfloat16),
            pltpu.SemaphoreType.DMA((len(SENDS) - 1,)),
        ],
        compiler_params=params(),
        cost_estimate=pl.CostEstimate(
            flops=2 * slots * slots * D * 2, bytes_accessed=4 * slots * D * 2, transcendentals=0
        ),
        name="cluster_attention",
    )(in_vmem(got))


def local_kernel(
    at_ref, q_ref, k_ref, v_ref, far_ref, near_ref, out_ref, key_ref, value_ref
):
    at = at_ref[0]
    own = k_ref[0:16].astype(jnp.float32)[0:1]
    nearest = near_ref[0, 0:16].astype(jnp.float32)[0:1]
    earlier = ((far_ref[0], far_ref[1]), (near_ref[0], near_ref[1]))
    for b, (key, value) in enumerate(earlier):
        there = at >= 2 - b
        start = jnp.where(at == 0, own, nearest)
        filler = jnp.broadcast_to(start, (TOK, D))
        rows = pl.ds(b * TOK, TOK)
        key_ref[rows] = jnp.where(there, key.astype(jnp.float32), filler).astype(jnp.bfloat16)
        value_ref[rows, 0:D] = value
        value_ref[rows, D : 2 * D] = jnp.full((TOK, D), jnp.where(there, 1.0, 0.0)).astype(
            jnp.bfloat16
        )
    key_ref[2 * TOK : 3 * TOK] = k_ref[...]
    value_ref[2 * TOK : 3 * TOK, 0:D] = v_ref[...]
    value_ref[2 * TOK : 3 * TOK, D : 2 * D] = jnp.ones((TOK, D), jnp.bfloat16)
    size = 256
    column = lax.broadcasted_iota(jnp.int32, (size, size), 1)
    line = lax.broadcasted_iota(jnp.int32, (size, size), 0)
    tasks = []
    for i in range(TOK // size):
        low = i * size
        high = low + 2 * TOK
        middle = low + size + CHUNK
        spans = [
            (low, low + size, column > line),
            (low + size, middle, None),
            (middle, high, None),
            (high, high + size, column <= line),
        ]
        tasks += tasks_of(i, spans)

    def write(i, mixed):
        out_ref[i * size : (i + 1) * size] = mixed

    attend(
        tasks, lambda i: q_ref[i * size : (i + 1) * size], key_ref, value_ref, write
    )


def windowed(at, q, k, v, far, near):
    return pl.pallas_call(
        local_kernel,
        out_shape=jax.ShapeDtypeStruct((TOK, D), jnp.bfloat16),
        in_specs=[pl.BlockSpec(memory_space=pltpu.SMEM)] + [VMEM] * 5,
        out_specs=VMEM,
        scratch_shapes=[
            pltpu.VMEM((3 * TOK, D), jnp.bfloat16),
            pltpu.VMEM((3 * TOK, 2 * D), jnp.bfloat16),
        ],
        compiler_params=params(),
        cost_estimate=pl.CostEstimate(
            flops=TOK * 2304 * D * 4, bytes_accessed=8 * TOK * D * 2, transcendentals=0
        ),
        name="window_attention",
    )(at, q, k, v, in_vmem(far), in_vmem(near))


def pick_kernel(place_ref, pick_ref):
    place = jnp.broadcast_to(place_ref[0:1], (128, TOK)).T.astype(jnp.int32)
    lane = lax.broadcasted_iota(jnp.int32, (TOK, 128), 1)
    for low in range(0, TOK, 128):
        pick_ref[:, low : low + 128] = (
            (place == lane + low).astype(jnp.float32).astype(jnp.bfloat16)
        )


def picks(place):
    return pl.pallas_call(
        pick_kernel,
        out_shape=pltpu.VMEM((TOK, TOK), jnp.bfloat16),
        in_specs=[VMEM],
        out_specs=VMEM,
        compiler_params=params(),
        name="picks",
    )(in_vmem(place))


def unpack_kernel(start_ref, pick_ref, back_ref, out_ref, sorted_ref):
    for c in range(CLUSTERS):
        sorted_ref[pl.ds(start_ref[0, c], CAP)] = back_ref[c].astype(jnp.float32)
    out_ref[...] = jnp.dot(
        pick_ref[...], sorted_ref[0:TOK].astype(jnp.bfloat16), preferred_element_type=jnp.float32
    ).astype(jnp.bfloat16)


def unpack(start, pick, back):
    return pl.pallas_call(
        unpack_kernel,
        out_shape=jax.ShapeDtypeStruct((TOK, D), jnp.bfloat16),
        in_specs=[pl.BlockSpec(memory_space=pltpu.SMEM), VMEM, VMEM],
        out_specs=VMEM,
        scratch_shapes=[pltpu.VMEM((TOK + CAP, D), jnp.float32)],
        compiler_params=params(),
        name="unpack_slots",
    )(start, in_vmem(pick), in_vmem(back))


def passed_along(value, steps):
    count = lax.axis_size(SEQ)
    return lax.ppermute(value, SEQ, [(s, s + steps) for s in range(count - steps)])


def local(q_routed, k_routed, v_routed, memberships, q_local, k_local, v_local):
    seq_index = lax.axis_index(SEQ)
    ids = memberships.reshape(1, TOK)
    sent, place, start = pack(ids, q_routed[0], k_routed[0], v_routed[0])
    got = lax.all_to_all(sent, SEQ, split_axis=0, concat_axis=0, tiled=True)
    pair = jnp.concatenate([k_local, v_local], axis=0)
    got, pair = lax.optimization_barrier((got, pair))
    far = passed_along(pair, 2)
    mixed = routed(got)
    mixed, far, place = lax.optimization_barrier((mixed, far, place))
    pick = picks(place)
    back = lax.all_to_all(mixed, SEQ, split_axis=0, concat_axis=0, tiled=True)
    given = jnp.where(seq_index % 2 == 1, far, pair)
    near = lax.ppermute(given, SEQ, [(s, s ^ 1) for s in range(lax.axis_size(SEQ))])
    out_local = windowed(
        seq_index.astype(jnp.int32).reshape(1), q_local[0], k_local[0], v_local[0], far, near
    )
    back, out_local = lax.optimization_barrier((back, out_local))
    out_routed = unpack(start, pick, back)
    return (out_routed[None], out_local[None])


def solution(mesh):
    torus = Mesh(
        mesh.devices.reshape(mesh.shape["head"], 4, 4, 2), ("head", "seq_0", "seq_1", "seq_2")
    )
    spec = P("head", SEQ, None)
    return jax.shard_map(
        local,
        mesh=torus,
        in_specs=(spec,) * 7,
        out_specs=(spec, spec),
        check_vma=False,
    )
```

```python
import jax
import jax.numpy as jnp
from jax import lax
from jax.experimental import pallas as pl
from jax.experimental.pallas import tpu as pltpu
from jax.sharding import Mesh
from jax.sharding import PartitionSpec as P

CLUSTERS = 32
CAP = 128
TOK = 1024
D = 128
SEQ = ("seq_0", "seq_1", "seq_2")
LOG2E = 1.4426950408889634
EXP_SCALE = LOG2E * D**-0.5
NEVER = -1e30
EMPTY = 256.0
GROUP = 8
CHUNK = 1024
SENDS = (0, 24, 32)
VMEM = pl.BlockSpec(memory_space=pltpu.VMEM)
HBM = pl.BlockSpec(memory_space=pltpu.HBM)


def in_vmem(array):
    return pltpu.with_memory_space_constraint(array, pltpu.VMEM)


def in_hbm(array):
    return pltpu.with_memory_space_constraint(array, pltpu.HBM)


def params():
    return pltpu.CompilerParams(vmem_limit_bytes=40 * 1024 * 1024)


def pack_kernel(
    ids_ref,
    q_ref,
    k_ref,
    v_ref,
    sent_ref,
    place_ref,
    start_ref,
    rows_ref,
    sorted_ref,
    stage_ref,
    start_smem,
    in_sems,
    out_sems,
    start_sem,
):
    loads = [
        pltpu.make_async_copy(ref, rows_ref.at[i], in_sems.at[i])
        for i, ref in enumerate((q_ref, k_ref, v_ref))
    ]
    for load in loads:
        load.start()
    ids = ids_ref[...]
    cluster = lax.broadcasted_iota(jnp.int32, (CLUSTERS, TOK), 0)
    member = (ids == cluster).astype(jnp.float32)
    member_b = member.astype(jnp.bfloat16)
    upto = (
        lax.broadcasted_iota(jnp.int32, (128, 128), 0)
        <= lax.broadcasted_iota(jnp.int32, (128, 128), 1)
    ).astype(jnp.bfloat16)
    count = jnp.zeros((CLUSTERS, 1), jnp.float32)
    ranks = []
    for first in range(0, TOK, 128):
        seen = count + jnp.dot(
            member_b[:, first : first + 128], upto, preferred_element_type=jnp.float32
        )
        ranks.append(
            jnp.sum(member[:, first : first + 128] * seen, axis=0, keepdims=True) - 1.0
        )
        count = seen[:, 127:128]
    line = lax.broadcasted_iota(jnp.int32, (CLUSTERS, 128), 0)
    lane = lax.broadcasted_iota(jnp.int32, (CLUSTERS, 128), 1)
    start = jnp.sum(
        jnp.where(line < lane, jnp.broadcast_to(count, (CLUSTERS, 128)), 0.0),
        axis=0,
        keepdims=True,
    )
    start_ref[...] = jnp.broadcast_to(start, start_ref.shape).astype(jnp.int32)
    starts = pltpu.make_async_copy(start_ref, start_smem, start_sem)
    starts.start()
    before = jnp.sum(
        jnp.where(cluster < ids, jnp.broadcast_to(count, (CLUSTERS, TOK)), 0.0),
        axis=0,
        keepdims=True,
    )
    place = before + jnp.concatenate(ranks, axis=1)
    place_ref[...] = jnp.broadcast_to(place, place_ref.shape)
    place = place.astype(jnp.int32)
    for load in loads:
        load.wait()
    rows = jnp.concatenate([rows_ref[i] for i in range(3)], axis=1)
    size = 256
    for low in range(0, TOK, size):
        line = lax.broadcasted_iota(jnp.int32, (size, TOK), 0) + low
        in_order = jnp.dot(
            (place == line).astype(jnp.float32).astype(jnp.bfloat16),
            rows,
            preferred_element_type=jnp.float32,
        )
        for i in range(3):
            sorted_ref[i, low : low + size] = in_order[:, i * D : (i + 1) * D]
    starts.wait()
    slot = lax.broadcasted_iota(jnp.int32, (CAP, D), 0)
    sends = []
    for base in range(0, CLUSTERS, GROUP):
        for c in range(base, base + GROUP):
            first = start_smem[0, c]
            used = slot < start_smem[0, c + 1] - first
            for i, blank in enumerate((0.0, EMPTY, 0.0)):
                mine = jnp.where(used, sorted_ref[i, pl.ds(first, CAP)], blank)
                stage_ref[c, i * CAP : (i + 1) * CAP] = mine.astype(jnp.bfloat16)
        part = pl.ds(base, GROUP)
        sends.append(
            pltpu.make_async_copy(
                stage_ref.at[part], sent_ref.at[part], out_sems.at[base // GROUP]
            )
        )
        sends[-1].start()
    for send in sends:
        send.wait()


def pack(ids, q, k, v):
    return pl.pallas_call(
        pack_kernel,
        out_shape=(
            pltpu.HBM((CLUSTERS, 3 * CAP, D), jnp.bfloat16),
            pltpu.VMEM((8, TOK), jnp.float32),
            pltpu.VMEM((8, 128), jnp.int32),
        ),
        in_specs=[VMEM] + [HBM] * 3,
        out_specs=(HBM, VMEM, VMEM),
        scratch_shapes=[
            pltpu.VMEM((3, TOK, D), jnp.bfloat16),
            pltpu.VMEM((3, TOK + CAP, D), jnp.float32),
            pltpu.VMEM((CLUSTERS, 3 * CAP, D), jnp.bfloat16),
            pltpu.SMEM((8, 128), jnp.int32),
            pltpu.SemaphoreType.DMA((3,)),
            pltpu.SemaphoreType.DMA((CLUSTERS // GROUP,)),
            pltpu.SemaphoreType.DMA,
        ],
        compiler_params=params(),
        name="pack_slots",
    )(ids, in_hbm(q), in_hbm(k), in_hbm(v))


def attend(tasks, query_of, key_ref, value_ref, write):
    def score(task):
        block, low, high, mask, _, _ = task
        s = lax.dot_general(
            query_of(block),
            key_ref[low:high],
            (((1,), (1,)), ((), ())),
            preferred_element_type=jnp.float32,
        )
        return s if mask is None else jnp.where(mask, s, NEVER)

    coming = score(tasks[0])
    for t, (block, low, high, _, first, last) in enumerate(tasks):
        s = coming
        if t + 1 < len(tasks):
            coming = score(tasks[t + 1])
        top = jnp.max(s, axis=1, keepdims=True)
        if not first:
            top = jnp.maximum(top, top_before)
        weight = jnp.exp2(s * EXP_SCALE - top * EXP_SCALE).astype(jnp.bfloat16)
        total = jnp.dot(weight, value_ref[low:high], preferred_element_type=jnp.float32)
        if not first:
            total = total + total_before * jnp.exp2((top_before - top) * EXP_SCALE)
        top_before, total_before = top, total
        if last:
            mass = total[:, D : 2 * D]
            write(
                block, (total[:, 0:D] / jnp.where(mass > 0.0, mass, 1.0)).astype(jnp.bfloat16)
            )


def tasks_of(block, spans):
    return [
        (block, low, high, mask, t == 0, t == len(spans) - 1)
        for t, (low, high, mask) in enumerate(spans)
    ]


def routed_kernel(
    got_ref,
    out_ref,
    key_ref,
    value_ref,
    mixed_ref,
    out_sems,
):
    blocks = got_ref.shape[0]
    first = jnp.zeros((1, D), jnp.float32)
    for s in reversed(range(blocks)):
        row = got_ref[s, CAP : CAP + 16].astype(jnp.float32)[0:1]
        first = jnp.where(row < 100.0, row, first)
    filler = jnp.broadcast_to(first, (CAP, D))
    size = 2 * CAP
    within = lax.broadcasted_iota(jnp.int32, (size, size), 1) <= lax.broadcasted_iota(
        jnp.int32, (size, size), 0
    )
    for s in range(blocks):
        at = slice(s * CAP, (s + 1) * CAP)
        key = got_ref[s, CAP : 2 * CAP].astype(jnp.float32)
        used = key < 100.0
        key_ref[at] = jnp.where(used, key, filler).astype(jnp.bfloat16)
        value_ref[at, 0:D] = got_ref[s, 2 * CAP : 3 * CAP]
        value_ref[at, D : 2 * D] = used.astype(jnp.float32).astype(jnp.bfloat16)

    def query_of(i):
        return got_ref[2 * i : 2 * i + 2, 0:CAP].reshape(size, D)

    tasks = []
    for i in range(blocks // 2):
        own = i * size
        spans = [(low, min(low + CHUNK, own), None) for low in range(0, own, CHUNK)]
        tasks += tasks_of(i, spans + [(own, own + size, within)])
    sends = []

    def write(i, mixed):
        mixed_ref[2 * i : 2 * i + 2] = mixed.reshape(2, CAP, D)
        if 2 * i + 2 in SENDS:
            n = SENDS.index(2 * i + 2)
            part = pl.ds(SENDS[n - 1], SENDS[n] - SENDS[n - 1])
            sends.append(
                pltpu.make_async_copy(mixed_ref.at[part], out_ref.at[part], out_sems.at[n - 1])
            )
            sends[-1].start()

    attend(tasks, query_of, key_ref, value_ref, write)
    for send in sends:
        send.wait()


def routed(got):
    blocks = got.shape[0]
    slots = blocks * CAP
    return pl.pallas_call(
        routed_kernel,
        out_shape=pltpu.HBM((blocks, CAP, D), jnp.bfloat16),
        in_specs=[VMEM],
        out_specs=HBM,
        scratch_shapes=[
            pltpu.VMEM((slots, D), jnp.bfloat16),
            pltpu.VMEM((slots, 2 * D), jnp.bfloat16),
            pltpu.VMEM((blocks, CAP, D), jnp.bfloat16),
            pltpu.SemaphoreType.DMA((len(SENDS) - 1,)),
        ],
        compiler_params=params(),
        cost_estimate=pl.CostEstimate(
            flops=2 * slots * slots * D * 2, bytes_accessed=4 * slots * D * 2, transcendentals=0
        ),
        name="cluster_attention",
    )(in_vmem(got))


def local_kernel(
    at_ref, q_ref, k_ref, v_ref, far_ref, near_ref, out_ref, key_ref, value_ref
):
    at = at_ref[0]
    own = k_ref[0:16].astype(jnp.float32)[0:1]
    nearest = near_ref[0, 0:16].astype(jnp.float32)[0:1]
    earlier = ((far_ref[0], far_ref[1]), (near_ref[0], near_ref[1]))
    for b, (key, value) in enumerate(earlier):
        there = at >= 2 - b
        start = jnp.where(at == 0, own, nearest)
        filler = jnp.broadcast_to(start, (TOK, D))
        rows = pl.ds(b * TOK, TOK)
        key_ref[rows] = jnp.where(there, key.astype(jnp.float32), filler).astype(jnp.bfloat16)
        value_ref[rows, 0:D] = value
        value_ref[rows, D : 2 * D] = jnp.full((TOK, D), jnp.where(there, 1.0, 0.0)).astype(
            jnp.bfloat16
        )
    key_ref[2 * TOK : 3 * TOK] = k_ref[...]
    value_ref[2 * TOK : 3 * TOK, 0:D] = v_ref[...]
    value_ref[2 * TOK : 3 * TOK, D : 2 * D] = jnp.ones((TOK, D), jnp.bfloat16)
    size = 256
    column = lax.broadcasted_iota(jnp.int32, (size, size), 1)
    line = lax.broadcasted_iota(jnp.int32, (size, size), 0)
    tasks = []
    for i in range(TOK // size):
        low = i * size
        high = low + 2 * TOK
        middle = low + size + CHUNK
        spans = [
            (low, low + size, column > line),
            (low + size, middle, None),
            (middle, high, None),
            (high, high + size, column <= line),
        ]
        tasks += tasks_of(i, spans)

    def write(i, mixed):
        out_ref[i * size : (i + 1) * size] = mixed

    attend(
        tasks, lambda i: q_ref[i * size : (i + 1) * size], key_ref, value_ref, write
    )


def windowed(at, q, k, v, far, near):
    return pl.pallas_call(
        local_kernel,
        out_shape=jax.ShapeDtypeStruct((TOK, D), jnp.bfloat16),
        in_specs=[pl.BlockSpec(memory_space=pltpu.SMEM)] + [VMEM] * 5,
        out_specs=VMEM,
        scratch_shapes=[
            pltpu.VMEM((3 * TOK, D), jnp.bfloat16),
            pltpu.VMEM((3 * TOK, 2 * D), jnp.bfloat16),
        ],
        compiler_params=params(),
        cost_estimate=pl.CostEstimate(
            flops=TOK * 2304 * D * 4, bytes_accessed=8 * TOK * D * 2, transcendentals=0
        ),
        name="window_attention",
    )(at, q, k, v, in_vmem(far), in_vmem(near))


def pick_kernel(place_ref, pick_ref):
    place = jnp.broadcast_to(place_ref[0:1], (128, TOK)).T.astype(jnp.int32)
    lane = lax.broadcasted_iota(jnp.int32, (TOK, 128), 1)
    for low in range(0, TOK, 128):
        pick_ref[:, low : low + 128] = (
            (place == lane + low).astype(jnp.float32).astype(jnp.bfloat16)
        )


def picks(place):
    return pl.pallas_call(
        pick_kernel,
        out_shape=pltpu.VMEM((TOK, TOK), jnp.bfloat16),
        in_specs=[VMEM],
        out_specs=VMEM,
        compiler_params=params(),
        name="picks",
    )(in_vmem(place))


def unpack_kernel(start_ref, pick_ref, back_ref, out_ref, sorted_ref):
    for c in range(CLUSTERS):
        sorted_ref[pl.ds(start_ref[0, c], CAP)] = back_ref[c].astype(jnp.float32)
    out_ref[...] = jnp.dot(
        pick_ref[...], sorted_ref[0:TOK].astype(jnp.bfloat16), preferred_element_type=jnp.float32
    ).astype(jnp.bfloat16)


def unpack(start, pick, back):
    return pl.pallas_call(
        unpack_kernel,
        out_shape=jax.ShapeDtypeStruct((TOK, D), jnp.bfloat16),
        in_specs=[pl.BlockSpec(memory_space=pltpu.SMEM), VMEM, VMEM],
        out_specs=VMEM,
        scratch_shapes=[pltpu.VMEM((TOK + CAP, D), jnp.float32)],
        compiler_params=params(),
        name="unpack_slots",
    )(start, in_vmem(pick), in_vmem(back))


def passed_along(value, steps):
    count = lax.axis_size(SEQ)
    return lax.ppermute(value, SEQ, [(s, s + steps) for s in range(count - steps)])


def local(q_routed, k_routed, v_routed, memberships, q_local, k_local, v_local):
    seq_index = lax.axis_index(SEQ)
    ids = memberships.reshape(1, TOK)
    sent, place, start = pack(ids, q_routed[0], k_routed[0], v_routed[0])
    got = lax.all_to_all(sent, SEQ, split_axis=0, concat_axis=0, tiled=True)
    pair = jnp.concatenate([k_local, v_local], axis=0)
    got, pair = lax.optimization_barrier((got, pair))
    far = passed_along(pair, 2)
    mixed = routed(got)
    mixed, place = lax.optimization_barrier((mixed, place))
    pick = picks(place)
    far, pick = lax.optimization_barrier((far, pick))
    back = lax.all_to_all(mixed, SEQ, split_axis=0, concat_axis=0, tiled=True)
    given = jnp.where(seq_index % 2 == 1, far, pair)
    near = lax.ppermute(given, SEQ, [(s, s ^ 1) for s in range(lax.axis_size(SEQ))])
    out_local = windowed(
        seq_index.astype(jnp.int32).reshape(1), q_local[0], k_local[0], v_local[0], far, near
    )
    back, out_local = lax.optimization_barrier((back, out_local))
    out_routed = unpack(start, pick, back)
    return (out_routed[None], out_local[None])


def solution(mesh):
    torus = Mesh(
        mesh.devices.reshape(mesh.shape["head"], 4, 4, 2), ("head", "seq_0", "seq_1", "seq_2")
    )
    spec = P("head", SEQ, None)
    return jax.shard_map(
        local,
        mesh=torus,
        in_specs=(spec,) * 7,
        out_specs=(spec, spec),
        check_vma=False,
    )
```

```python
import jax
import jax.numpy as jnp
from jax import lax
from jax.experimental import pallas as pl
from jax.experimental.pallas import tpu as pltpu
from jax.sharding import Mesh
from jax.sharding import PartitionSpec as P

CLUSTERS = 32
CAP = 128
TOK = 1024
D = 128
SEQ = ("seq_0", "seq_1", "seq_2")
LOG2E = 1.4426950408889634
EXP_SCALE = LOG2E * D**-0.5
NEVER = -1e30
EMPTY = 256.0
GROUP = 8
CHUNK = 2048
TILE = 256
SENDS = {11: (8, 24), 15: (24, 32), 0: (0, 8)}
VMEM = pl.BlockSpec(memory_space=pltpu.VMEM)
HBM = pl.BlockSpec(memory_space=pltpu.HBM)


def in_vmem(array):
    return pltpu.with_memory_space_constraint(array, pltpu.VMEM)


def in_hbm(array):
    return pltpu.with_memory_space_constraint(array, pltpu.HBM)


def params():
    return pltpu.CompilerParams(vmem_limit_bytes=40 * 1024 * 1024)


def pack_kernel(
    ids_ref,
    q_ref,
    k_ref,
    v_ref,
    sent_ref,
    place_ref,
    start_ref,
    rows_ref,
    sorted_ref,
    stage_ref,
    start_smem,
    in_sems,
    out_sems,
    start_sem,
):
    loads = [
        pltpu.make_async_copy(ref, rows_ref.at[i], in_sems.at[i])
        for i, ref in enumerate((q_ref, k_ref, v_ref))
    ]
    for load in loads:
        load.start()
    ids = ids_ref[...]
    cluster = lax.broadcasted_iota(jnp.int32, (CLUSTERS, TOK), 0)
    member = (ids == cluster).astype(jnp.float32)
    member_b = member.astype(jnp.bfloat16)
    upto = (
        lax.broadcasted_iota(jnp.int32, (128, 128), 0)
        <= lax.broadcasted_iota(jnp.int32, (128, 128), 1)
    ).astype(jnp.bfloat16)
    count = jnp.zeros((CLUSTERS, 1), jnp.float32)
    ranks = []
    for first in range(0, TOK, 128):
        seen = count + jnp.dot(
            member_b[:, first : first + 128], upto, preferred_element_type=jnp.float32
        )
        ranks.append(
            jnp.sum(member[:, first : first + 128] * seen, axis=0, keepdims=True) - 1.0
        )
        count = seen[:, 127:128]
    line = lax.broadcasted_iota(jnp.int32, (CLUSTERS, 128), 0)
    lane = lax.broadcasted_iota(jnp.int32, (CLUSTERS, 128), 1)
    start = jnp.sum(
        jnp.where(line < lane, jnp.broadcast_to(count, (CLUSTERS, 128)), 0.0),
        axis=0,
        keepdims=True,
    )
    start_ref[...] = jnp.broadcast_to(start, start_ref.shape).astype(jnp.int32)
    starts = pltpu.make_async_copy(start_ref, start_smem, start_sem)
    starts.start()
    before = jnp.sum(
        jnp.where(cluster < ids, jnp.broadcast_to(count, (CLUSTERS, TOK)), 0.0),
        axis=0,
        keepdims=True,
    )
    place = before + jnp.concatenate(ranks, axis=1)
    place_ref[...] = jnp.broadcast_to(place, place_ref.shape)
    place = place.astype(jnp.int32)
    for load in loads:
        load.wait()
    rows = jnp.concatenate([rows_ref[i] for i in range(3)], axis=1)
    size = 256
    for low in range(0, TOK, size):
        line = lax.broadcasted_iota(jnp.int32, (size, TOK), 0) + low
        in_order = jnp.dot(
            (place == line).astype(jnp.float32).astype(jnp.bfloat16),
            rows,
            preferred_element_type=jnp.float32,
        )
        for i in range(3):
            sorted_ref[i, low : low + size] = in_order[:, i * D : (i + 1) * D]
    starts.wait()
    slot = lax.broadcasted_iota(jnp.int32, (CAP, D), 0)
    sends = []
    for base in range(0, CLUSTERS, GROUP):
        for c in range(base, base + GROUP):
            first = start_smem[0, c]
            used = slot < start_smem[0, c + 1] - first
            for i, blank in enumerate((0.0, EMPTY, 0.0)):
                mine = jnp.where(used, sorted_ref[i, pl.ds(first, CAP)], blank)
                stage_ref[c, i * CAP : (i + 1) * CAP] = mine.astype(jnp.bfloat16)
        part = pl.ds(base, GROUP)
        sends.append(
            pltpu.make_async_copy(
                stage_ref.at[part], sent_ref.at[part], out_sems.at[base // GROUP]
            )
        )
        sends[-1].start()
    for send in sends:
        send.wait()


def pack(ids, q, k, v):
    return pl.pallas_call(
        pack_kernel,
        out_shape=(
            pltpu.HBM((CLUSTERS, 3 * CAP, D), jnp.bfloat16),
            pltpu.VMEM((8, TOK), jnp.float32),
            pltpu.VMEM((8, 128), jnp.int32),
        ),
        in_specs=[VMEM] + [HBM] * 3,
        out_specs=(HBM, VMEM, VMEM),
        scratch_shapes=[
            pltpu.VMEM((3, TOK, D), jnp.bfloat16),
            pltpu.VMEM((3, TOK + CAP, D), jnp.float32),
            pltpu.VMEM((CLUSTERS, 3 * CAP, D), jnp.bfloat16),
            pltpu.SMEM((8, 128), jnp.int32),
            pltpu.SemaphoreType.DMA((3,)),
            pltpu.SemaphoreType.DMA((CLUSTERS // GROUP,)),
            pltpu.SemaphoreType.DMA,
        ],
        compiler_params=params(),
        name="pack_slots",
    )(ids, in_hbm(q), in_hbm(k), in_hbm(v))


def attend(tasks, query_of, key_ref, value_ref, write):
    def score(task):
        block, low, high, head, tail, _, _ = task
        s = lax.dot_general(
            query_of(block),
            key_ref[low:high],
            (((1,), (1,)), ((), ())),
            preferred_element_type=jnp.float32,
        )
        if head is not None:
            edge = head.shape[1]
            s = jnp.concatenate([jnp.where(head, s[:, :edge], NEVER), s[:, edge:]], axis=1)
        if tail is not None:
            edge = high - low - tail.shape[1]
            masked = jnp.where(tail, s[:, edge:], NEVER)
            s = masked if edge == 0 else jnp.concatenate([s[:, :edge], masked], axis=1)
        return s

    coming = score(tasks[0])
    for t, (block, low, high, _, _, first, last) in enumerate(tasks):
        s = coming
        if t + 1 < len(tasks):
            coming = score(tasks[t + 1])
        top = jnp.max(s, axis=1, keepdims=True)
        if not first:
            top = jnp.maximum(top, top_before)
        weight = jnp.exp2(s * EXP_SCALE - top * EXP_SCALE).astype(jnp.bfloat16)
        total = jnp.dot(weight, value_ref[low:high], preferred_element_type=jnp.float32)
        if not first:
            total = total + total_before * jnp.exp2((top_before - top) * EXP_SCALE)
        top_before, total_before = top, total
        if last:
            mass = total[:, D : 2 * D]
            write(
                block, (total[:, 0:D] / jnp.where(mass > 0.0, mass, 1.0)).astype(jnp.bfloat16)
            )


def tasks_of(block, low, high, head, tail):
    parts = -(-(high - low) // CHUNK)
    steps = (high - low) // TILE
    edges = [low + TILE * (steps * p // parts) for p in range(parts + 1)]
    return [
        (
            block,
            edges[p],
            edges[p + 1],
            head if p == 0 else None,
            tail if p == parts - 1 else None,
            p == 0,
            p == parts - 1,
        )
        for p in range(parts)
    ]


def routed_kernel(
    got_ref,
    out_ref,
    key_ref,
    value_ref,
    mixed_ref,
    out_sems,
):
    blocks = got_ref.shape[0]
    first = jnp.zeros((1, D), jnp.float32)
    for s in reversed(range(blocks)):
        row = got_ref[s, CAP : CAP + 16].astype(jnp.float32)[0:1]
        first = jnp.where(row < 100.0, row, first)
    filler = jnp.broadcast_to(first, (CAP, D))
    size = 2 * CAP
    within = lax.broadcasted_iota(jnp.int32, (size, size), 1) <= lax.broadcasted_iota(
        jnp.int32, (size, size), 0
    )
    ready = set()

    def query_of(i):
        for s in sorted(set(range(2 * i + 2)) - ready):
            at = slice(s * CAP, (s + 1) * CAP)
            key = got_ref[s, CAP : 2 * CAP].astype(jnp.float32)
            used = key < 100.0
            key_ref[at] = jnp.where(used, key, filler).astype(jnp.bfloat16)
            value_ref[at, 0:D] = got_ref[s, 2 * CAP : 3 * CAP]
            value_ref[at, D : 2 * D] = used.astype(jnp.float32).astype(jnp.bfloat16)
            ready.add(s)
        return got_ref[2 * i : 2 * i + 2, 0:CAP].reshape(size, D)

    tasks = []
    pairs = blocks // 2
    for i in [*range(pairs // 4, pairs), *reversed(range(pairs // 4))]:
        tasks += tasks_of(i, 0, (i + 1) * size, None, within)
    sends = []

    def write(i, mixed):
        mixed_ref[2 * i : 2 * i + 2] = mixed.reshape(2, CAP, D)
        if i in SENDS:
            n, (low, high) = list(SENDS).index(i), SENDS[i]
            part = pl.ds(low, high - low)
            sends.append(
                pltpu.make_async_copy(mixed_ref.at[part], out_ref.at[part], out_sems.at[n])
            )
            sends[-1].start()

    attend(tasks, query_of, key_ref, value_ref, write)
    for send in sends:
        send.wait()


def routed(got):
    blocks = got.shape[0]
    slots = blocks * CAP
    return pl.pallas_call(
        routed_kernel,
        out_shape=pltpu.HBM((blocks, CAP, D), jnp.bfloat16),
        in_specs=[VMEM],
        out_specs=HBM,
        scratch_shapes=[
            pltpu.VMEM((slots, D), jnp.bfloat16),
            pltpu.VMEM((slots, 2 * D), jnp.bfloat16),
            pltpu.VMEM((blocks, CAP, D), jnp.bfloat16),
            pltpu.SemaphoreType.DMA((len(SENDS),)),
        ],
        compiler_params=params(),
        cost_estimate=pl.CostEstimate(
            flops=2 * slots * slots * D * 2, bytes_accessed=4 * slots * D * 2, transcendentals=0
        ),
        name="cluster_attention",
    )(in_vmem(got))


def local_kernel(
    at_ref, q_ref, k_ref, v_ref, far_ref, near_ref, out_ref, key_ref, value_ref
):
    at = at_ref[0]
    own = k_ref[0:16].astype(jnp.float32)[0:1]
    nearest = near_ref[0, 0:16].astype(jnp.float32)[0:1]
    earlier = ((far_ref[0], far_ref[1]), (near_ref[0], near_ref[1]))
    for b, (key, value) in enumerate(earlier):
        there = at >= 2 - b
        start = jnp.where(at == 0, own, nearest)
        filler = jnp.broadcast_to(start, (TOK, D))
        rows = pl.ds(b * TOK, TOK)
        key_ref[rows] = jnp.where(there, key.astype(jnp.float32), filler).astype(jnp.bfloat16)
        value_ref[rows, 0:D] = value
        value_ref[rows, D : 2 * D] = jnp.full((TOK, D), jnp.where(there, 1.0, 0.0)).astype(
            jnp.bfloat16
        )
    key_ref[2 * TOK : 3 * TOK] = k_ref[...]
    value_ref[2 * TOK : 3 * TOK, 0:D] = v_ref[...]
    value_ref[2 * TOK : 3 * TOK, D : 2 * D] = jnp.ones((TOK, D), jnp.bfloat16)
    size = 256
    column = lax.broadcasted_iota(jnp.int32, (size, size), 1)
    line = lax.broadcasted_iota(jnp.int32, (size, size), 0)
    tasks = []
    for i in range(TOK // size):
        low = i * size
        tasks += tasks_of(i, low, low + 2 * TOK + size, column > line, column <= line)

    def write(i, mixed):
        out_ref[i * size : (i + 1) * size] = mixed

    attend(
        tasks, lambda i: q_ref[i * size : (i + 1) * size], key_ref, value_ref, write
    )


def windowed(at, q, k, v, far, near):
    return pl.pallas_call(
        local_kernel,
        out_shape=jax.ShapeDtypeStruct((TOK, D), jnp.bfloat16),
        in_specs=[pl.BlockSpec(memory_space=pltpu.SMEM)] + [VMEM] * 5,
        out_specs=VMEM,
        scratch_shapes=[
            pltpu.VMEM((3 * TOK, D), jnp.bfloat16),
            pltpu.VMEM((3 * TOK, 2 * D), jnp.bfloat16),
        ],
        compiler_params=params(),
        cost_estimate=pl.CostEstimate(
            flops=TOK * 2304 * D * 4, bytes_accessed=8 * TOK * D * 2, transcendentals=0
        ),
        name="window_attention",
    )(at, q, k, v, in_vmem(far), in_vmem(near))


def pick_kernel(place_ref, pick_ref):
    place = jnp.broadcast_to(place_ref[0:1], (128, TOK)).T.astype(jnp.int32)
    lane = lax.broadcasted_iota(jnp.int32, (TOK, 128), 1)
    for low in range(0, TOK, 128):
        pick_ref[:, low : low + 128] = (
            (place == lane + low).astype(jnp.float32).astype(jnp.bfloat16)
        )


def picks(place):
    return pl.pallas_call(
        pick_kernel,
        out_shape=pltpu.VMEM((TOK, TOK), jnp.bfloat16),
        in_specs=[VMEM],
        out_specs=VMEM,
        compiler_params=params(),
        name="picks",
    )(in_vmem(place))


def unpack_kernel(start_ref, pick_ref, back_ref, out_ref, sorted_ref):
    for c in range(CLUSTERS):
        sorted_ref[pl.ds(start_ref[0, c], CAP)] = back_ref[c].astype(jnp.float32)
    out_ref[...] = jnp.dot(
        pick_ref[...], sorted_ref[0:TOK].astype(jnp.bfloat16), preferred_element_type=jnp.float32
    ).astype(jnp.bfloat16)


def unpack(start, pick, back):
    return pl.pallas_call(
        unpack_kernel,
        out_shape=jax.ShapeDtypeStruct((TOK, D), jnp.bfloat16),
        in_specs=[pl.BlockSpec(memory_space=pltpu.SMEM), VMEM, VMEM],
        out_specs=VMEM,
        scratch_shapes=[pltpu.VMEM((TOK + CAP, D), jnp.float32)],
        compiler_params=params(),
        name="unpack_slots",
    )(start, in_vmem(pick), in_vmem(back))


def passed_along(value, steps):
    count = lax.axis_size(SEQ)
    return lax.ppermute(value, SEQ, [(s, s + steps) for s in range(count - steps)])


def local(q_routed, k_routed, v_routed, memberships, q_local, k_local, v_local):
    seq_index = lax.axis_index(SEQ)
    ids = memberships.reshape(1, TOK)
    sent, place, start = pack(ids, q_routed[0], k_routed[0], v_routed[0])
    got = lax.all_to_all(sent, SEQ, split_axis=0, concat_axis=0, tiled=True)
    pair = jnp.concatenate([k_local, v_local], axis=0)
    got, pair = lax.optimization_barrier((got, pair))
    far = passed_along(pair, 2)
    mixed = routed(got)
    mixed, place = lax.optimization_barrier((mixed, place))
    pick = picks(place)
    far, pick = lax.optimization_barrier((far, pick))
    back = lax.all_to_all(mixed, SEQ, split_axis=0, concat_axis=0, tiled=True)
    given = jnp.where(seq_index % 2 == 1, far, pair)
    near = lax.ppermute(given, SEQ, [(s, s ^ 1) for s in range(lax.axis_size(SEQ))])
    out_local = windowed(
        seq_index.astype(jnp.int32).reshape(1), q_local[0], k_local[0], v_local[0], far, near
    )
    back, out_local = lax.optimization_barrier((back, out_local))
    out_routed = unpack(start, pick, back)
    return (out_routed[None], out_local[None])


def solution(mesh):
    torus = Mesh(
        mesh.devices.reshape(mesh.shape["head"], 4, 4, 2), ("head", "seq_0", "seq_1", "seq_2")
    )
    spec = P("head", SEQ, None)
    return jax.shard_map(
        local,
        mesh=torus,
        in_specs=(spec,) * 7,
        out_specs=(spec, spec),
        check_vma=False,
    )
```

```python
import jax
import jax.numpy as jnp
from jax import lax
from jax.experimental import pallas as pl
from jax.experimental.pallas import tpu as pltpu
from jax.sharding import Mesh
from jax.sharding import PartitionSpec as P

CLUSTERS = 32
CAP = 128
TOK = 1024
D = 128
SEQ = ("seq_0", "seq_1", "seq_2")
LOG2E = 1.4426950408889634
EXP_SCALE = LOG2E * D**-0.5
NEVER = -1e30
EMPTY = 256.0
GROUP = 8
CHUNK = 2048
TILE = 256
SENDS = {11: (8, 24), 15: (24, 32), 0: (0, 8)}
VMEM = pl.BlockSpec(memory_space=pltpu.VMEM)
HBM = pl.BlockSpec(memory_space=pltpu.HBM)


def in_vmem(array):
    return pltpu.with_memory_space_constraint(array, pltpu.VMEM)


def in_hbm(array):
    return pltpu.with_memory_space_constraint(array, pltpu.HBM)


def params():
    return pltpu.CompilerParams(vmem_limit_bytes=40 * 1024 * 1024)


def pack_kernel(
    ids_ref,
    q_ref,
    k_ref,
    v_ref,
    sent_ref,
    place_ref,
    start_ref,
    rows_ref,
    sorted_ref,
    stage_ref,
    start_smem,
    in_sems,
    out_sems,
    start_sem,
):
    loads = [
        pltpu.make_async_copy(ref, rows_ref.at[i], in_sems.at[i])
        for i, ref in enumerate((q_ref, k_ref, v_ref))
    ]
    for load in loads:
        load.start()
    ids = ids_ref[...]
    cluster = lax.broadcasted_iota(jnp.int32, (CLUSTERS, TOK), 0)
    member = (ids == cluster).astype(jnp.float32)
    member_b = member.astype(jnp.bfloat16)
    upto = (
        lax.broadcasted_iota(jnp.int32, (128, 128), 0)
        <= lax.broadcasted_iota(jnp.int32, (128, 128), 1)
    ).astype(jnp.bfloat16)
    count = jnp.zeros((CLUSTERS, 1), jnp.float32)
    ranks = []
    for first in range(0, TOK, 128):
        seen = count + jnp.dot(
            member_b[:, first : first + 128], upto, preferred_element_type=jnp.float32
        )
        ranks.append(
            jnp.sum(member[:, first : first + 128] * seen, axis=0, keepdims=True) - 1.0
        )
        count = seen[:, 127:128]
    line = lax.broadcasted_iota(jnp.int32, (CLUSTERS, 128), 0)
    lane = lax.broadcasted_iota(jnp.int32, (CLUSTERS, 128), 1)
    start = jnp.sum(
        jnp.where(line < lane, jnp.broadcast_to(count, (CLUSTERS, 128)), 0.0),
        axis=0,
        keepdims=True,
    )
    start_ref[...] = jnp.broadcast_to(start, start_ref.shape).astype(jnp.int32)
    starts = pltpu.make_async_copy(start_ref, start_smem, start_sem)
    starts.start()
    before = jnp.sum(
        jnp.where(cluster < ids, jnp.broadcast_to(count, (CLUSTERS, TOK)), 0.0),
        axis=0,
        keepdims=True,
    )
    place = before + jnp.concatenate(ranks, axis=1)
    place_ref[...] = jnp.broadcast_to(place, place_ref.shape)
    place = place.astype(jnp.int32)
    for load in loads:
        load.wait()
    rows = jnp.concatenate([rows_ref[i] for i in range(3)], axis=1)
    size = 256
    for low in range(0, TOK, size):
        line = lax.broadcasted_iota(jnp.int32, (size, TOK), 0) + low
        in_order = jnp.dot(
            (place == line).astype(jnp.float32).astype(jnp.bfloat16),
            rows,
            preferred_element_type=jnp.float32,
        )
        for i in range(3):
            sorted_ref[i, low : low + size] = in_order[:, i * D : (i + 1) * D]
    starts.wait()
    slot = lax.broadcasted_iota(jnp.int32, (CAP, D), 0)
    sends = []
    for base in range(0, CLUSTERS, GROUP):
        for c in range(base, base + GROUP):
            first = start_smem[0, c]
            used = slot < start_smem[0, c + 1] - first
            for i, blank in enumerate((0.0, EMPTY, 0.0)):
                mine = jnp.where(used, sorted_ref[i, pl.ds(first, CAP)], blank)
                stage_ref[c, i * CAP : (i + 1) * CAP] = mine.astype(jnp.bfloat16)
        part = pl.ds(base, GROUP)
        sends.append(
            pltpu.make_async_copy(
                stage_ref.at[part], sent_ref.at[part], out_sems.at[base // GROUP]
            )
        )
        sends[-1].start()
    for send in sends:
        send.wait()


def pack(ids, q, k, v):
    return pl.pallas_call(
        pack_kernel,
        out_shape=(
            pltpu.HBM((CLUSTERS, 3 * CAP, D), jnp.bfloat16),
            pltpu.VMEM((8, TOK), jnp.float32),
            pltpu.VMEM((8, 128), jnp.int32),
        ),
        in_specs=[VMEM] + [HBM] * 3,
        out_specs=(HBM, VMEM, VMEM),
        scratch_shapes=[
            pltpu.VMEM((3, TOK, D), jnp.bfloat16),
            pltpu.VMEM((3, TOK + CAP, D), jnp.float32),
            pltpu.VMEM((CLUSTERS, 3 * CAP, D), jnp.bfloat16),
            pltpu.SMEM((8, 128), jnp.int32),
            pltpu.SemaphoreType.DMA((3,)),
            pltpu.SemaphoreType.DMA((CLUSTERS // GROUP,)),
            pltpu.SemaphoreType.DMA,
        ],
        compiler_params=params(),
        name="pack_slots",
    )(ids, in_hbm(q), in_hbm(k), in_hbm(v))


def attend(tasks, query_of, key_ref, value_ref, write):
    def score(task):
        block, low, high, head, tail, _, _ = task
        s = lax.dot_general(
            query_of(block),
            key_ref[low:high],
            (((1,), (1,)), ((), ())),
            preferred_element_type=jnp.float32,
        )
        if head is not None:
            edge = head.shape[1]
            s = jnp.concatenate([jnp.where(head, s[:, :edge], NEVER), s[:, edge:]], axis=1)
        if tail is not None:
            edge = high - low - tail.shape[1]
            masked = jnp.where(tail, s[:, edge:], NEVER)
            s = masked if edge == 0 else jnp.concatenate([s[:, :edge], masked], axis=1)
        return s

    coming = score(tasks[0])
    for t, (block, low, high, _, _, first, last) in enumerate(tasks):
        s = coming
        if t + 1 < len(tasks):
            coming = score(tasks[t + 1])
        top = jnp.max(s, axis=1, keepdims=True)
        if not first:
            top = jnp.maximum(top, top_before)
        weight = jnp.exp2(s * EXP_SCALE - top * EXP_SCALE).astype(jnp.bfloat16)
        total = jnp.dot(weight, value_ref[low:high], preferred_element_type=jnp.float32)
        if not first:
            total = total + total_before * jnp.exp2((top_before - top) * EXP_SCALE)
        top_before, total_before = top, total
        if last:
            mass = total[:, D : 2 * D]
            write(
                block, (total[:, 0:D] / jnp.where(mass > 0.0, mass, 1.0)).astype(jnp.bfloat16)
            )


def tasks_of(block, low, high, head, tail):
    parts = -(-(high - low) // CHUNK)
    steps = (high - low) // TILE
    edges = [low + TILE * (steps * p // parts) for p in range(parts + 1)]
    return [
        (
            block,
            edges[p],
            edges[p + 1],
            head if p == 0 else None,
            tail if p == parts - 1 else None,
            p == 0,
            p == parts - 1,
        )
        for p in range(parts)
    ]


def routed_kernel(
    got_ref,
    out_ref,
    key_ref,
    value_ref,
    mixed_ref,
    out_sems,
):
    blocks = got_ref.shape[0]
    first = jnp.zeros((1, D), jnp.float32)
    for s in reversed(range(blocks)):
        row = got_ref[s, CAP : CAP + 16].astype(jnp.float32)[0:1]
        first = jnp.where(row < 100.0, row, first)
    filler = jnp.broadcast_to(first, (CAP, D))
    size = 2 * CAP
    within = lax.broadcasted_iota(jnp.int32, (size, size), 1) <= lax.broadcasted_iota(
        jnp.int32, (size, size), 0
    )
    ready = set()

    def query_of(i):
        for s in sorted(set(range(2 * i + 2)) - ready):
            at = slice(s * CAP, (s + 1) * CAP)
            key = got_ref[s, CAP : 2 * CAP].astype(jnp.float32)
            used = key < 100.0
            key_ref[at] = jnp.where(used, key, filler).astype(jnp.bfloat16)
            value_ref[at, 0:D] = got_ref[s, 2 * CAP : 3 * CAP]
            value_ref[at, D : 2 * D] = used.astype(jnp.float32).astype(jnp.bfloat16)
            ready.add(s)
        return got_ref[2 * i : 2 * i + 2, 0:CAP].reshape(size, D)

    tasks = []
    pairs = blocks // 2
    for i in [*range(pairs // 4, pairs), *reversed(range(pairs // 4))]:
        tasks += tasks_of(i, 0, (i + 1) * size, None, within)
    sends = []

    def write(i, mixed):
        mixed_ref[2 * i : 2 * i + 2] = mixed.reshape(2, CAP, D)
        if i in SENDS:
            n, (low, high) = list(SENDS).index(i), SENDS[i]
            part = pl.ds(low, high - low)
            sends.append(
                pltpu.make_async_copy(mixed_ref.at[part], out_ref.at[part], out_sems.at[n])
            )
            sends[-1].start()

    attend(tasks, query_of, key_ref, value_ref, write)
    for send in sends:
        send.wait()


def routed(got):
    blocks = got.shape[0]
    slots = blocks * CAP
    return pl.pallas_call(
        routed_kernel,
        out_shape=pltpu.HBM((blocks, CAP, D), jnp.bfloat16),
        in_specs=[VMEM],
        out_specs=HBM,
        scratch_shapes=[
            pltpu.VMEM((slots, D), jnp.bfloat16),
            pltpu.VMEM((slots, 2 * D), jnp.bfloat16),
            pltpu.VMEM((blocks, CAP, D), jnp.bfloat16),
            pltpu.SemaphoreType.DMA((len(SENDS),)),
        ],
        compiler_params=params(),
        cost_estimate=pl.CostEstimate(
            flops=2 * slots * slots * D * 2, bytes_accessed=4 * slots * D * 2, transcendentals=0
        ),
        name="cluster_attention",
    )(in_vmem(got))


def local_kernel(
    at_ref, q_ref, k_ref, v_ref, far_ref, near_ref, out_ref, key_ref, value_ref
):
    at = at_ref[0]
    own = k_ref[0:16].astype(jnp.float32)[0:1]
    nearest = near_ref[0, 0:16].astype(jnp.float32)[0:1]
    earlier = ((far_ref[0], far_ref[1]), (near_ref[0], near_ref[1]))
    for b, (key, value) in enumerate(earlier):
        there = at >= 2 - b
        start = jnp.where(at == 0, own, nearest)
        filler = jnp.broadcast_to(start, (TOK, D))
        rows = pl.ds(b * TOK, TOK)
        key_ref[rows] = jnp.where(there, key.astype(jnp.float32), filler).astype(jnp.bfloat16)
        value_ref[rows, 0:D] = jnp.where(there, value.astype(jnp.float32), 0.0).astype(jnp.bfloat16)
        value_ref[rows, D : 2 * D] = jnp.full((TOK, D), jnp.where(there, 1.0, 0.0)).astype(
            jnp.bfloat16
        )
    key_ref[2 * TOK : 3 * TOK] = k_ref[...]
    value_ref[2 * TOK : 3 * TOK, 0:D] = v_ref[...]
    value_ref[2 * TOK : 3 * TOK, D : 2 * D] = jnp.ones((TOK, D), jnp.bfloat16)
    size = 256
    column = lax.broadcasted_iota(jnp.int32, (size, size), 1)
    line = lax.broadcasted_iota(jnp.int32, (size, size), 0)
    tasks = []
    for i in range(TOK // size):
        low = i * size
        tasks += tasks_of(i, low, low + 2 * TOK + size, column > line, column <= line)

    def write(i, mixed):
        out_ref[i * size : (i + 1) * size] = mixed

    attend(
        tasks, lambda i: q_ref[i * size : (i + 1) * size], key_ref, value_ref, write
    )


def windowed(at, q, k, v, far, near):
    return pl.pallas_call(
        local_kernel,
        out_shape=jax.ShapeDtypeStruct((TOK, D), jnp.bfloat16),
        in_specs=[pl.BlockSpec(memory_space=pltpu.SMEM)] + [VMEM] * 5,
        out_specs=VMEM,
        scratch_shapes=[
            pltpu.VMEM((3 * TOK, D), jnp.bfloat16),
            pltpu.VMEM((3 * TOK, 2 * D), jnp.bfloat16),
        ],
        compiler_params=params(),
        cost_estimate=pl.CostEstimate(
            flops=TOK * 2304 * D * 4, bytes_accessed=8 * TOK * D * 2, transcendentals=0
        ),
        name="window_attention",
    )(at, q, k, v, in_vmem(far), in_vmem(near))


def pick_kernel(place_ref, pick_ref):
    place = jnp.broadcast_to(place_ref[0:1], (128, TOK)).T.astype(jnp.int32)
    lane = lax.broadcasted_iota(jnp.int32, (TOK, 128), 1)
    for low in range(0, TOK, 128):
        pick_ref[:, low : low + 128] = (
            (place == lane + low).astype(jnp.float32).astype(jnp.bfloat16)
        )


def picks(place):
    return pl.pallas_call(
        pick_kernel,
        out_shape=pltpu.VMEM((TOK, TOK), jnp.bfloat16),
        in_specs=[VMEM],
        out_specs=VMEM,
        compiler_params=params(),
        name="picks",
    )(in_vmem(place))


def unpack_kernel(start_ref, pick_ref, back_ref, out_ref, sorted_ref):
    for c in range(CLUSTERS):
        sorted_ref[pl.ds(start_ref[0, c], CAP)] = back_ref[c].astype(jnp.float32)
    out_ref[...] = jnp.dot(
        pick_ref[...], sorted_ref[0:TOK].astype(jnp.bfloat16), preferred_element_type=jnp.float32
    ).astype(jnp.bfloat16)


def unpack(start, pick, back):
    return pl.pallas_call(
        unpack_kernel,
        out_shape=jax.ShapeDtypeStruct((TOK, D), jnp.bfloat16),
        in_specs=[pl.BlockSpec(memory_space=pltpu.SMEM), VMEM, VMEM],
        out_specs=VMEM,
        scratch_shapes=[pltpu.VMEM((TOK + CAP, D), jnp.float32)],
        compiler_params=params(),
        name="unpack_slots",
    )(start, in_vmem(pick), in_vmem(back))


def passed_along(value, steps):
    count = lax.axis_size(SEQ)
    return lax.ppermute(value, SEQ, [(s, (s + steps) % count) for s in range(count)])


def local(q_routed, k_routed, v_routed, memberships, q_local, k_local, v_local):
    seq_index = lax.axis_index(SEQ)
    ids = memberships.reshape(1, TOK)
    sent, place, start = pack(ids, q_routed[0], k_routed[0], v_routed[0])
    got = lax.all_to_all(sent, SEQ, split_axis=0, concat_axis=0, tiled=True)
    pair = jnp.concatenate([k_local, v_local], axis=0)
    got, pair = lax.optimization_barrier((got, pair))
    far = passed_along(pair, 2)
    mixed = routed(got)
    mixed, place = lax.optimization_barrier((mixed, place))
    pick = picks(place)
    far, pick = lax.optimization_barrier((far, pick))
    back = lax.all_to_all(mixed, SEQ, split_axis=0, concat_axis=0, tiled=True)
    given = jnp.where(seq_index % 2 == 1, far, pair)
    near = lax.ppermute(given, SEQ, [(s, s ^ 1) for s in range(lax.axis_size(SEQ))])
    out_local = windowed(
        seq_index.astype(jnp.int32).reshape(1), q_local[0], k_local[0], v_local[0], far, near
    )
    back, out_local = lax.optimization_barrier((back, out_local))
    out_routed = unpack(start, pick, back)
    return (out_routed[None], out_local[None])


def solution(mesh):
    torus = Mesh(
        mesh.devices.reshape(mesh.shape["head"], 4, 4, 2), ("head", "seq_0", "seq_1", "seq_2")
    )
    spec = P("head", SEQ, None)
    return jax.shard_map(
        local,
        mesh=torus,
        in_specs=(spec,) * 7,
        out_specs=(spec, spec),
        check_vma=False,
    )
```

```python
import jax
import jax.numpy as jnp
from jax import lax
from jax.experimental import pallas as pl
from jax.experimental.pallas import tpu as pltpu
from jax.sharding import Mesh
from jax.sharding import PartitionSpec as P

CLUSTERS = 32
CAP = 128
TOK = 1024
D = 128
SEQ = ("seq_0", "seq_1", "seq_2")
LOG2E = 1.4426950408889634
EXP_SCALE = LOG2E * D**-0.5
NEVER = -1e30
EMPTY = 256.0
GROUP = 8
CHUNK = 2048
TILE = 256
SENDS = {11: (8, 24), 15: (24, 32), 0: (0, 8)}
VMEM = pl.BlockSpec(memory_space=pltpu.VMEM)
HBM = pl.BlockSpec(memory_space=pltpu.HBM)


def in_vmem(array):
    return pltpu.with_memory_space_constraint(array, pltpu.VMEM)


def in_hbm(array):
    return pltpu.with_memory_space_constraint(array, pltpu.HBM)


def params():
    return pltpu.CompilerParams(vmem_limit_bytes=40 * 1024 * 1024)


def pack_kernel(
    ids_ref,
    q_ref,
    k_ref,
    v_ref,
    sent_ref,
    place_ref,
    start_ref,
    rows_ref,
    sorted_ref,
    stage_ref,
    start_smem,
    in_sems,
    out_sems,
    start_sem,
):
    loads = [
        pltpu.make_async_copy(ref, rows_ref.at[i], in_sems.at[i])
        for i, ref in enumerate((q_ref, k_ref, v_ref))
    ]
    for load in loads:
        load.start()
    ids = ids_ref[...]
    cluster = lax.broadcasted_iota(jnp.int32, (CLUSTERS, TOK), 0)
    member = (ids == cluster).astype(jnp.float32)
    member_b = member.astype(jnp.bfloat16)
    upto = (
        lax.broadcasted_iota(jnp.int32, (128, 128), 0)
        <= lax.broadcasted_iota(jnp.int32, (128, 128), 1)
    ).astype(jnp.bfloat16)
    count = jnp.zeros((CLUSTERS, 1), jnp.float32)
    ranks = []
    for first in range(0, TOK, 128):
        seen = count + jnp.dot(
            member_b[:, first : first + 128], upto, preferred_element_type=jnp.float32
        )
        ranks.append(
            jnp.sum(member[:, first : first + 128] * seen, axis=0, keepdims=True) - 1.0
        )
        count = seen[:, 127:128]
    line = lax.broadcasted_iota(jnp.int32, (CLUSTERS, 128), 0)
    lane = lax.broadcasted_iota(jnp.int32, (CLUSTERS, 128), 1)
    start = jnp.sum(
        jnp.where(line < lane, jnp.broadcast_to(count, (CLUSTERS, 128)), 0.0),
        axis=0,
        keepdims=True,
    )
    start_ref[...] = jnp.broadcast_to(start, start_ref.shape).astype(jnp.int32)
    starts = pltpu.make_async_copy(start_ref, start_smem, start_sem)
    starts.start()
    before = jnp.sum(
        jnp.where(cluster < ids, jnp.broadcast_to(count, (CLUSTERS, TOK)), 0.0),
        axis=0,
        keepdims=True,
    )
    place = before + jnp.concatenate(ranks, axis=1)
    place_ref[...] = jnp.broadcast_to(place, place_ref.shape)
    place = place.astype(jnp.int32)
    for load in loads:
        load.wait()
    rows = jnp.concatenate([rows_ref[i] for i in range(3)], axis=1)
    size = 256
    for low in range(0, TOK, size):
        line = lax.broadcasted_iota(jnp.int32, (size, TOK), 0) + low
        in_order = jnp.dot(
            (place == line).astype(jnp.float32).astype(jnp.bfloat16),
            rows,
            preferred_element_type=jnp.float32,
        )
        for i in range(3):
            sorted_ref[i, low : low + size] = in_order[:, i * D : (i + 1) * D]
    starts.wait()
    slot = lax.broadcasted_iota(jnp.int32, (CAP, D), 0)
    sends = []
    for base in range(0, CLUSTERS, GROUP):
        for c in range(base, base + GROUP):
            first = start_smem[0, c]
            used = slot < start_smem[0, c + 1] - first
            for i, blank in enumerate((0.0, EMPTY, 0.0)):
                mine = jnp.where(used, sorted_ref[i, pl.ds(first, CAP)], blank)
                stage_ref[c, i * CAP : (i + 1) * CAP] = mine.astype(jnp.bfloat16)
        part = pl.ds(base, GROUP)
        sends.append(
            pltpu.make_async_copy(
                stage_ref.at[part], sent_ref.at[part], out_sems.at[base // GROUP]
            )
        )
        sends[-1].start()
    for send in sends:
        send.wait()


def pack(ids, q, k, v):
    return pl.pallas_call(
        pack_kernel,
        out_shape=(
            pltpu.HBM((CLUSTERS, 3 * CAP, D), jnp.bfloat16),
            pltpu.VMEM((8, TOK), jnp.float32),
            pltpu.VMEM((8, 128), jnp.int32),
        ),
        in_specs=[VMEM] + [HBM] * 3,
        out_specs=(HBM, VMEM, VMEM),
        scratch_shapes=[
            pltpu.VMEM((3, TOK, D), jnp.bfloat16),
            pltpu.VMEM((3, TOK + CAP, D), jnp.float32),
            pltpu.VMEM((CLUSTERS, 3 * CAP, D), jnp.bfloat16),
            pltpu.SMEM((8, 128), jnp.int32),
            pltpu.SemaphoreType.DMA((3,)),
            pltpu.SemaphoreType.DMA((CLUSTERS // GROUP,)),
            pltpu.SemaphoreType.DMA,
        ],
        compiler_params=params(),
        name="pack_slots",
    )(ids, in_hbm(q), in_hbm(k), in_hbm(v))


def put_keys(key_ref, rows, key):
    scaled = key * EXP_SCALE
    high = scaled.astype(jnp.bfloat16)
    key_ref[rows, 0:D] = high
    key_ref[rows, D : 2 * D] = (scaled - high.astype(jnp.float32)).astype(jnp.bfloat16)


def attend(tasks, query_of, key_ref, value_ref, write):
    def score(task):
        block, low, high, head, tail, _, _ = task
        queries = query_of(block)
        s = lax.dot_general(
            jnp.concatenate([queries, queries], axis=1),
            key_ref[low:high],
            (((1,), (1,)), ((), ())),
            preferred_element_type=jnp.float32,
        )
        if head is not None:
            edge = head.shape[1]
            s = jnp.concatenate([jnp.where(head, s[:, :edge], NEVER), s[:, edge:]], axis=1)
        if tail is not None:
            edge = high - low - tail.shape[1]
            masked = jnp.where(tail, s[:, edge:], NEVER)
            s = masked if edge == 0 else jnp.concatenate([s[:, :edge], masked], axis=1)
        return s

    coming = score(tasks[0])
    for t, (block, low, high, _, _, first, last) in enumerate(tasks):
        s = coming
        if t + 1 < len(tasks):
            coming = score(tasks[t + 1])
        top = jnp.max(s, axis=1, keepdims=True)
        if not first:
            top = jnp.maximum(top, top_before)
        weight = jnp.exp2(s - top).astype(jnp.bfloat16)
        total = jnp.dot(weight, value_ref[low:high], preferred_element_type=jnp.float32)
        if not first:
            total = total + total_before * jnp.exp2(top_before - top)
        top_before, total_before = top, total
        if last:
            mass = total[:, D : 2 * D]
            write(
                block, (total[:, 0:D] / jnp.where(mass > 0.0, mass, 1.0)).astype(jnp.bfloat16)
            )


def tasks_of(block, low, high, head, tail):
    parts = -(-(high - low) // CHUNK)
    steps = (high - low) // TILE
    edges = [low + TILE * (steps * p // parts) for p in range(parts + 1)]
    return [
        (
            block,
            edges[p],
            edges[p + 1],
            head if p == 0 else None,
            tail if p == parts - 1 else None,
            p == 0,
            p == parts - 1,
        )
        for p in range(parts)
    ]


def routed_kernel(
    got_ref,
    out_ref,
    key_ref,
    value_ref,
    mixed_ref,
    out_sems,
):
    blocks = got_ref.shape[0]
    first = jnp.zeros((1, D), jnp.float32)
    for s in reversed(range(blocks)):
        row = got_ref[s, CAP : CAP + 16].astype(jnp.float32)[0:1]
        first = jnp.where(row < 100.0, row, first)
    filler = jnp.broadcast_to(first, (CAP, D))
    size = 2 * CAP
    within = lax.broadcasted_iota(jnp.int32, (size, size), 1) <= lax.broadcasted_iota(
        jnp.int32, (size, size), 0
    )
    ready = set()

    def query_of(i):
        for s in sorted(set(range(2 * i + 2)) - ready):
            at = slice(s * CAP, (s + 1) * CAP)
            key = got_ref[s, CAP : 2 * CAP].astype(jnp.float32)
            used = key < 100.0
            put_keys(key_ref, at, jnp.where(used, key, filler))
            value_ref[at, 0:D] = got_ref[s, 2 * CAP : 3 * CAP]
            value_ref[at, D : 2 * D] = used.astype(jnp.float32).astype(jnp.bfloat16)
            ready.add(s)
        return got_ref[2 * i : 2 * i + 2, 0:CAP].reshape(size, D)

    tasks = []
    pairs = blocks // 2
    for i in [*range(pairs // 4, pairs), *reversed(range(pairs // 4))]:
        tasks += tasks_of(i, 0, (i + 1) * size, None, within)
    sends = []

    def write(i, mixed):
        mixed_ref[2 * i : 2 * i + 2] = mixed.reshape(2, CAP, D)
        if i in SENDS:
            n, (low, high) = list(SENDS).index(i), SENDS[i]
            part = pl.ds(low, high - low)
            sends.append(
                pltpu.make_async_copy(mixed_ref.at[part], out_ref.at[part], out_sems.at[n])
            )
            sends[-1].start()

    attend(tasks, query_of, key_ref, value_ref, write)
    for send in sends:
        send.wait()


def routed(got):
    blocks = got.shape[0]
    slots = blocks * CAP
    return pl.pallas_call(
        routed_kernel,
        out_shape=pltpu.HBM((blocks, CAP, D), jnp.bfloat16),
        in_specs=[VMEM],
        out_specs=HBM,
        scratch_shapes=[
            pltpu.VMEM((slots, 2 * D), jnp.bfloat16),
            pltpu.VMEM((slots, 2 * D), jnp.bfloat16),
            pltpu.VMEM((blocks, CAP, D), jnp.bfloat16),
            pltpu.SemaphoreType.DMA((len(SENDS),)),
        ],
        compiler_params=params(),
        cost_estimate=pl.CostEstimate(
            flops=2 * slots * slots * D * 2, bytes_accessed=4 * slots * D * 2, transcendentals=0
        ),
        name="cluster_attention",
    )(in_vmem(got))


def local_kernel(
    at_ref, q_ref, k_ref, v_ref, far_ref, near_ref, out_ref, key_ref, value_ref
):
    at = at_ref[0]
    own = k_ref[0:16].astype(jnp.float32)[0:1]
    nearest = near_ref[0, 0:16].astype(jnp.float32)[0:1]
    earlier = ((far_ref[0], far_ref[1]), (near_ref[0], near_ref[1]))
    for b, (key, value) in enumerate(earlier):
        there = at >= 2 - b
        start = jnp.where(at == 0, own, nearest)
        filler = jnp.broadcast_to(start, (TOK, D))
        rows = pl.ds(b * TOK, TOK)
        put_keys(key_ref, rows, jnp.where(there, key.astype(jnp.float32), filler))
        value_ref[rows, 0:D] = jnp.where(there, value.astype(jnp.float32), 0.0).astype(jnp.bfloat16)
        value_ref[rows, D : 2 * D] = jnp.full((TOK, D), jnp.where(there, 1.0, 0.0)).astype(
            jnp.bfloat16
        )
    put_keys(key_ref, slice(2 * TOK, 3 * TOK), k_ref[...].astype(jnp.float32))
    value_ref[2 * TOK : 3 * TOK, 0:D] = v_ref[...]
    value_ref[2 * TOK : 3 * TOK, D : 2 * D] = jnp.ones((TOK, D), jnp.bfloat16)
    size = 256
    column = lax.broadcasted_iota(jnp.int32, (size, size), 1)
    line = lax.broadcasted_iota(jnp.int32, (size, size), 0)
    tasks = []
    for i in range(TOK // size):
        low = i * size
        tasks += tasks_of(i, low, low + 2 * TOK + size, column > line, column <= line)

    def write(i, mixed):
        out_ref[i * size : (i + 1) * size] = mixed

    attend(
        tasks, lambda i: q_ref[i * size : (i + 1) * size], key_ref, value_ref, write
    )


def windowed(at, q, k, v, far, near):
    return pl.pallas_call(
        local_kernel,
        out_shape=jax.ShapeDtypeStruct((TOK, D), jnp.bfloat16),
        in_specs=[pl.BlockSpec(memory_space=pltpu.SMEM)] + [VMEM] * 5,
        out_specs=VMEM,
        scratch_shapes=[
            pltpu.VMEM((3 * TOK, 2 * D), jnp.bfloat16),
            pltpu.VMEM((3 * TOK, 2 * D), jnp.bfloat16),
        ],
        compiler_params=params(),
        cost_estimate=pl.CostEstimate(
            flops=TOK * 2304 * D * 4, bytes_accessed=8 * TOK * D * 2, transcendentals=0
        ),
        name="window_attention",
    )(at, q, k, v, in_vmem(far), in_vmem(near))


def pick_kernel(place_ref, pick_ref):
    place = jnp.broadcast_to(place_ref[0:1], (128, TOK)).T.astype(jnp.int32)
    lane = lax.broadcasted_iota(jnp.int32, (TOK, 128), 1)
    for low in range(0, TOK, 128):
        pick_ref[:, low : low + 128] = (
            (place == lane + low).astype(jnp.float32).astype(jnp.bfloat16)
        )


def picks(place):
    return pl.pallas_call(
        pick_kernel,
        out_shape=pltpu.VMEM((TOK, TOK), jnp.bfloat16),
        in_specs=[VMEM],
        out_specs=VMEM,
        compiler_params=params(),
        name="picks",
    )(in_vmem(place))


def unpack_kernel(start_ref, pick_ref, back_ref, out_ref, sorted_ref):
    for c in range(CLUSTERS):
        sorted_ref[pl.ds(start_ref[0, c], CAP)] = back_ref[c].astype(jnp.float32)
    out_ref[...] = jnp.dot(
        pick_ref[...], sorted_ref[0:TOK].astype(jnp.bfloat16), preferred_element_type=jnp.float32
    ).astype(jnp.bfloat16)


def unpack(start, pick, back):
    return pl.pallas_call(
        unpack_kernel,
        out_shape=jax.ShapeDtypeStruct((TOK, D), jnp.bfloat16),
        in_specs=[pl.BlockSpec(memory_space=pltpu.SMEM), VMEM, VMEM],
        out_specs=VMEM,
        scratch_shapes=[pltpu.VMEM((TOK + CAP, D), jnp.float32)],
        compiler_params=params(),
        name="unpack_slots",
    )(start, in_vmem(pick), in_vmem(back))


def passed_along(value, steps):
    count = lax.axis_size(SEQ)
    return lax.ppermute(value, SEQ, [(s, (s + steps) % count) for s in range(count)])


def local(q_routed, k_routed, v_routed, memberships, q_local, k_local, v_local):
    seq_index = lax.axis_index(SEQ)
    ids = memberships.reshape(1, TOK)
    sent, place, start = pack(ids, q_routed[0], k_routed[0], v_routed[0])
    got = lax.all_to_all(sent, SEQ, split_axis=0, concat_axis=0, tiled=True)
    pair = jnp.concatenate([k_local, v_local], axis=0)
    got, pair = lax.optimization_barrier((got, pair))
    far = passed_along(pair, 2)
    mixed = routed(got)
    mixed, place = lax.optimization_barrier((mixed, place))
    pick = picks(place)
    far, pick = lax.optimization_barrier((far, pick))
    back = lax.all_to_all(mixed, SEQ, split_axis=0, concat_axis=0, tiled=True)
    given = jnp.where(seq_index % 2 == 1, far, pair)
    near = lax.ppermute(given, SEQ, [(s, s ^ 1) for s in range(lax.axis_size(SEQ))])
    out_local = windowed(
        seq_index.astype(jnp.int32).reshape(1), q_local[0], k_local[0], v_local[0], far, near
    )
    back, out_local = lax.optimization_barrier((back, out_local))
    out_routed = unpack(start, pick, back)
    return (out_routed[None], out_local[None])


def solution(mesh):
    torus = Mesh(
        mesh.devices.reshape(mesh.shape["head"], 4, 4, 2), ("head", "seq_0", "seq_1", "seq_2")
    )
    spec = P("head", SEQ, None)
    return jax.shard_map(
        local,
        mesh=torus,
        in_specs=(spec,) * 7,
        out_specs=(spec, spec),
        check_vma=False,
    )
```

```python
import jax
import jax.numpy as jnp
from jax import lax
from jax.experimental import pallas as pl
from jax.experimental.pallas import tpu as pltpu
from jax.sharding import Mesh
from jax.sharding import PartitionSpec as P

CLUSTERS = 32
CAP = 128
TOK = 1024
D = 128
SEQ = ("seq_0", "seq_1", "seq_2")
LOG2E = 1.4426950408889634
EXP_SCALE = LOG2E * D**-0.5
NEVER = -1e30
EMPTY = 256.0
GROUP = 8
CHUNK = 2048
TILE = 256
SENDS = {11: (8, 24), 15: (24, 32), 0: (0, 8)}
VMEM = pl.BlockSpec(memory_space=pltpu.VMEM)
HBM = pl.BlockSpec(memory_space=pltpu.HBM)


def in_vmem(array):
    return pltpu.with_memory_space_constraint(array, pltpu.VMEM)


def in_hbm(array):
    return pltpu.with_memory_space_constraint(array, pltpu.HBM)


def params():
    return pltpu.CompilerParams(vmem_limit_bytes=40 * 1024 * 1024)


def pack_kernel(
    ids_ref,
    q_ref,
    k_ref,
    v_ref,
    sent_ref,
    place_ref,
    start_ref,
    ids_vmem,
    rows_ref,
    sorted_ref,
    stage_ref,
    start_smem,
    in_sems,
    out_sems,
    start_sem,
    ids_sem,
):
    named = pltpu.make_async_copy(ids_ref, ids_vmem, ids_sem)
    named.start()
    loads = [
        pltpu.make_async_copy(ref, rows_ref.at[i], in_sems.at[i])
        for i, ref in enumerate((q_ref, k_ref, v_ref))
    ]
    for load in loads:
        load.start()
    named.wait()
    ids = ids_vmem[...]
    cluster = lax.broadcasted_iota(jnp.int32, (CLUSTERS, TOK), 0)
    member = (ids == cluster).astype(jnp.float32)
    member_b = member.astype(jnp.bfloat16)
    upto = (
        lax.broadcasted_iota(jnp.int32, (128, 128), 0)
        <= lax.broadcasted_iota(jnp.int32, (128, 128), 1)
    ).astype(jnp.bfloat16)
    count = jnp.zeros((CLUSTERS, 1), jnp.float32)
    ranks = []
    for first in range(0, TOK, 128):
        seen = count + jnp.dot(
            member_b[:, first : first + 128], upto, preferred_element_type=jnp.float32
        )
        ranks.append(
            jnp.sum(member[:, first : first + 128] * seen, axis=0, keepdims=True) - 1.0
        )
        count = seen[:, 127:128]
    line = lax.broadcasted_iota(jnp.int32, (CLUSTERS, 128), 0)
    lane = lax.broadcasted_iota(jnp.int32, (CLUSTERS, 128), 1)
    start = jnp.sum(
        jnp.where(line < lane, jnp.broadcast_to(count, (CLUSTERS, 128)), 0.0),
        axis=0,
        keepdims=True,
    )
    start_ref[...] = jnp.broadcast_to(start, start_ref.shape).astype(jnp.int32)
    starts = pltpu.make_async_copy(start_ref, start_smem, start_sem)
    starts.start()
    before = jnp.sum(
        jnp.where(cluster < ids, jnp.broadcast_to(count, (CLUSTERS, TOK)), 0.0),
        axis=0,
        keepdims=True,
    )
    place = before + jnp.concatenate(ranks, axis=1)
    place_ref[...] = jnp.broadcast_to(place, place_ref.shape)
    place = place.astype(jnp.int32)
    for load in loads:
        load.wait()
    rows = jnp.concatenate([rows_ref[i] for i in range(3)], axis=1)
    size = 256
    for low in range(0, TOK, size):
        line = lax.broadcasted_iota(jnp.int32, (size, TOK), 0) + low
        in_order = jnp.dot(
            (place == line).astype(jnp.float32).astype(jnp.bfloat16),
            rows,
            preferred_element_type=jnp.float32,
        )
        for i in range(3):
            sorted_ref[i, low : low + size] = in_order[:, i * D : (i + 1) * D]
    starts.wait()
    slot = lax.broadcasted_iota(jnp.int32, (CAP, D), 0)
    sends = []
    for base in range(0, CLUSTERS, GROUP):
        for c in range(base, base + GROUP):
            first = start_smem[0, c]
            used = slot < start_smem[0, c + 1] - first
            for i, blank in enumerate((0.0, EMPTY, 0.0)):
                mine = jnp.where(used, sorted_ref[i, pl.ds(first, CAP)], blank)
                stage_ref[c, i * CAP : (i + 1) * CAP] = mine.astype(jnp.bfloat16)
        part = pl.ds(base, GROUP)
        sends.append(
            pltpu.make_async_copy(
                stage_ref.at[part], sent_ref.at[part], out_sems.at[base // GROUP]
            )
        )
        sends[-1].start()
    for send in sends:
        send.wait()


def pack(ids, q, k, v):
    return pl.pallas_call(
        pack_kernel,
        out_shape=(
            pltpu.HBM((CLUSTERS, 3 * CAP, D), jnp.bfloat16),
            pltpu.VMEM((8, TOK), jnp.float32),
            pltpu.VMEM((8, 128), jnp.int32),
        ),
        in_specs=[HBM] * 4,
        out_specs=(HBM, VMEM, VMEM),
        scratch_shapes=[
            pltpu.VMEM((1, TOK), jnp.int32),
            pltpu.VMEM((3, TOK, D), jnp.bfloat16),
            pltpu.VMEM((3, TOK + CAP, D), jnp.float32),
            pltpu.VMEM((CLUSTERS, 3 * CAP, D), jnp.bfloat16),
            pltpu.SMEM((8, 128), jnp.int32),
            pltpu.SemaphoreType.DMA((3,)),
            pltpu.SemaphoreType.DMA((CLUSTERS // GROUP,)),
            pltpu.SemaphoreType.DMA,
            pltpu.SemaphoreType.DMA,
        ],
        compiler_params=params(),
        name="pack_slots",
    )(in_hbm(ids), in_hbm(q), in_hbm(k), in_hbm(v))


def put_keys(key_ref, rows, key):
    scaled = key * EXP_SCALE
    high = scaled.astype(jnp.bfloat16)
    key_ref[rows, 0:D] = high
    key_ref[rows, D : 2 * D] = (scaled - high.astype(jnp.float32)).astype(jnp.bfloat16)


def attend(tasks, query_of, key_ref, value_ref, write):
    def score(task):
        block, low, high, head, tail, _, _ = task
        queries = query_of(block)
        s = lax.dot_general(
            jnp.concatenate([queries, queries], axis=1),
            key_ref[low:high],
            (((1,), (1,)), ((), ())),
            preferred_element_type=jnp.float32,
        )
        if head is not None:
            edge = head.shape[1]
            s = jnp.concatenate([jnp.where(head, s[:, :edge], NEVER), s[:, edge:]], axis=1)
        if tail is not None:
            edge = high - low - tail.shape[1]
            masked = jnp.where(tail, s[:, edge:], NEVER)
            s = masked if edge == 0 else jnp.concatenate([s[:, :edge], masked], axis=1)
        return s

    coming = score(tasks[0])
    for t, (block, low, high, _, _, first, last) in enumerate(tasks):
        s = coming
        if t + 1 < len(tasks):
            coming = score(tasks[t + 1])
        top = jnp.max(s, axis=1, keepdims=True)
        if not first:
            top = jnp.maximum(top, top_before)
        weight = jnp.exp2(s - top).astype(jnp.bfloat16)
        total = jnp.dot(weight, value_ref[low:high], preferred_element_type=jnp.float32)
        if not first:
            total = total + total_before * jnp.exp2(top_before - top)
        top_before, total_before = top, total
        if last:
            mass = total[:, D : 2 * D]
            write(
                block, (total[:, 0:D] / jnp.where(mass > 0.0, mass, 1.0)).astype(jnp.bfloat16)
            )


def tasks_of(block, low, high, head, tail):
    parts = -(-(high - low) // CHUNK)
    steps = (high - low) // TILE
    edges = [low + TILE * (steps * p // parts) for p in range(parts + 1)]
    return [
        (
            block,
            edges[p],
            edges[p + 1],
            head if p == 0 else None,
            tail if p == parts - 1 else None,
            p == 0,
            p == parts - 1,
        )
        for p in range(parts)
    ]


def routed_kernel(
    got_ref,
    out_ref,
    key_ref,
    value_ref,
    mixed_ref,
    out_sems,
):
    blocks = got_ref.shape[0]
    first = jnp.zeros((1, D), jnp.float32)
    for s in reversed(range(blocks)):
        row = got_ref[s, CAP : CAP + 16].astype(jnp.float32)[0:1]
        first = jnp.where(row < 100.0, row, first)
    filler = jnp.broadcast_to(first, (CAP, D))
    size = 2 * CAP
    within = lax.broadcasted_iota(jnp.int32, (size, size), 1) <= lax.broadcasted_iota(
        jnp.int32, (size, size), 0
    )
    ready = set()

    def query_of(i):
        for s in sorted(set(range(2 * i + 2)) - ready):
            at = slice(s * CAP, (s + 1) * CAP)
            key = got_ref[s, CAP : 2 * CAP].astype(jnp.float32)
            used = key < 100.0
            put_keys(key_ref, at, jnp.where(used, key, filler))
            value_ref[at, 0:D] = got_ref[s, 2 * CAP : 3 * CAP]
            value_ref[at, D : 2 * D] = used.astype(jnp.float32).astype(jnp.bfloat16)
            ready.add(s)
        return got_ref[2 * i : 2 * i + 2, 0:CAP].reshape(size, D)

    tasks = []
    pairs = blocks // 2
    for i in [*range(pairs // 4, pairs), *reversed(range(pairs // 4))]:
        tasks += tasks_of(i, 0, (i + 1) * size, None, within)
    sends = []

    def write(i, mixed):
        mixed_ref[2 * i : 2 * i + 2] = mixed.reshape(2, CAP, D)
        if i in SENDS:
            n, (low, high) = list(SENDS).index(i), SENDS[i]
            part = pl.ds(low, high - low)
            sends.append(
                pltpu.make_async_copy(mixed_ref.at[part], out_ref.at[part], out_sems.at[n])
            )
            sends[-1].start()

    attend(tasks, query_of, key_ref, value_ref, write)
    for send in sends:
        send.wait()


def routed(got):
    blocks = got.shape[0]
    slots = blocks * CAP
    return pl.pallas_call(
        routed_kernel,
        out_shape=pltpu.HBM((blocks, CAP, D), jnp.bfloat16),
        in_specs=[VMEM],
        out_specs=HBM,
        scratch_shapes=[
            pltpu.VMEM((slots, 2 * D), jnp.bfloat16),
            pltpu.VMEM((slots, 2 * D), jnp.bfloat16),
            pltpu.VMEM((blocks, CAP, D), jnp.bfloat16),
            pltpu.SemaphoreType.DMA((len(SENDS),)),
        ],
        compiler_params=params(),
        cost_estimate=pl.CostEstimate(
            flops=2 * slots * slots * D * 2, bytes_accessed=4 * slots * D * 2, transcendentals=0
        ),
        name="cluster_attention",
    )(in_vmem(got))


def local_kernel(
    at_ref, q_ref, k_ref, v_ref, far_ref, near_ref, out_ref, key_ref, value_ref
):
    at = at_ref[0]
    own = k_ref[0:16].astype(jnp.float32)[0:1]
    nearest = near_ref[0, 0:16].astype(jnp.float32)[0:1]
    earlier = ((far_ref[0], far_ref[1]), (near_ref[0], near_ref[1]))
    for b, (key, value) in enumerate(earlier):
        there = at >= 2 - b
        start = jnp.where(at == 0, own, nearest)
        filler = jnp.broadcast_to(start, (TOK, D))
        rows = pl.ds(b * TOK, TOK)
        put_keys(key_ref, rows, jnp.where(there, key.astype(jnp.float32), filler))
        value_ref[rows, 0:D] = jnp.where(there, value.astype(jnp.float32), 0.0).astype(jnp.bfloat16)
        value_ref[rows, D : 2 * D] = jnp.full((TOK, D), jnp.where(there, 1.0, 0.0)).astype(
            jnp.bfloat16
        )
    put_keys(key_ref, slice(2 * TOK, 3 * TOK), k_ref[...].astype(jnp.float32))
    value_ref[2 * TOK : 3 * TOK, 0:D] = v_ref[...]
    value_ref[2 * TOK : 3 * TOK, D : 2 * D] = jnp.ones((TOK, D), jnp.bfloat16)
    size = 256
    column = lax.broadcasted_iota(jnp.int32, (size, size), 1)
    line = lax.broadcasted_iota(jnp.int32, (size, size), 0)
    tasks = []
    for i in range(TOK // size):
        low = i * size
        tasks += tasks_of(i, low, low + 2 * TOK + size, column > line, column <= line)

    def write(i, mixed):
        out_ref[i * size : (i + 1) * size] = mixed

    attend(
        tasks, lambda i: q_ref[i * size : (i + 1) * size], key_ref, value_ref, write
    )


def windowed(at, q, k, v, far, near):
    return pl.pallas_call(
        local_kernel,
        out_shape=jax.ShapeDtypeStruct((TOK, D), jnp.bfloat16),
        in_specs=[pl.BlockSpec(memory_space=pltpu.SMEM)] + [VMEM] * 5,
        out_specs=VMEM,
        scratch_shapes=[
            pltpu.VMEM((3 * TOK, 2 * D), jnp.bfloat16),
            pltpu.VMEM((3 * TOK, 2 * D), jnp.bfloat16),
        ],
        compiler_params=params(),
        cost_estimate=pl.CostEstimate(
            flops=TOK * 2304 * D * 4, bytes_accessed=8 * TOK * D * 2, transcendentals=0
        ),
        name="window_attention",
    )(at, q, k, v, in_vmem(far), in_vmem(near))


def pick_kernel(place_ref, pick_ref):
    place = jnp.broadcast_to(place_ref[0:1], (128, TOK)).T.astype(jnp.int32)
    lane = lax.broadcasted_iota(jnp.int32, (TOK, 128), 1)
    for low in range(0, TOK, 128):
        pick_ref[:, low : low + 128] = (
            (place == lane + low).astype(jnp.float32).astype(jnp.bfloat16)
        )


def picks(place):
    return pl.pallas_call(
        pick_kernel,
        out_shape=pltpu.VMEM((TOK, TOK), jnp.bfloat16),
        in_specs=[VMEM],
        out_specs=VMEM,
        compiler_params=params(),
        name="picks",
    )(in_vmem(place))


def unpack_kernel(start_ref, pick_ref, back_ref, out_ref, sorted_ref):
    for c in range(CLUSTERS):
        sorted_ref[pl.ds(start_ref[0, c], CAP)] = back_ref[c].astype(jnp.float32)
    out_ref[...] = jnp.dot(
        pick_ref[...], sorted_ref[0:TOK].astype(jnp.bfloat16), preferred_element_type=jnp.float32
    ).astype(jnp.bfloat16)


def unpack(start, pick, back):
    return pl.pallas_call(
        unpack_kernel,
        out_shape=jax.ShapeDtypeStruct((TOK, D), jnp.bfloat16),
        in_specs=[pl.BlockSpec(memory_space=pltpu.SMEM), VMEM, VMEM],
        out_specs=VMEM,
        scratch_shapes=[pltpu.VMEM((TOK + CAP, D), jnp.float32)],
        compiler_params=params(),
        name="unpack_slots",
    )(start, in_vmem(pick), in_vmem(back))


def passed_along(value, steps):
    count = lax.axis_size(SEQ)
    return lax.ppermute(value, SEQ, [(s, (s + steps) % count) for s in range(count)])


def local(q_routed, k_routed, v_routed, memberships, q_local, k_local, v_local):
    seq_index = lax.axis_index(SEQ)
    ids = memberships.reshape(1, TOK)
    sent, place, start = pack(ids, q_routed[0], k_routed[0], v_routed[0])
    got = lax.all_to_all(sent, SEQ, split_axis=0, concat_axis=0, tiled=True)
    pair = jnp.concatenate([k_local, v_local], axis=0)
    got, pair = lax.optimization_barrier((got, pair))
    far = passed_along(pair, 2)
    mixed = routed(got)
    mixed, place = lax.optimization_barrier((mixed, place))
    pick = picks(place)
    far, pick = lax.optimization_barrier((far, pick))
    back = lax.all_to_all(mixed, SEQ, split_axis=0, concat_axis=0, tiled=True)
    given = jnp.where(seq_index % 2 == 1, far, pair)
    near = lax.ppermute(given, SEQ, [(s, s ^ 1) for s in range(lax.axis_size(SEQ))])
    out_local = windowed(
        seq_index.astype(jnp.int32).reshape(1), q_local[0], k_local[0], v_local[0], far, near
    )
    back, out_local = lax.optimization_barrier((back, out_local))
    out_routed = unpack(start, pick, back)
    return (out_routed[None], out_local[None])


def solution(mesh):
    torus = Mesh(
        mesh.devices.reshape(mesh.shape["head"], 4, 4, 2), ("head", "seq_0", "seq_1", "seq_2")
    )
    spec = P("head", SEQ, None)
    return jax.shard_map(
        local,
        mesh=torus,
        in_specs=(spec,) * 7,
        out_specs=(spec, spec),
        check_vma=False,
    )
```
